512 devices in a mesh: outer: 8 (over y_hi, x), dp: 64 (over y_lo, z, core).
Axes of the slice: x: 4, y: 4 (y_hi: 2, y_lo: 2; y = y_hi * 2 + y_lo), z: 16, core: 2. Of those that a mesh axis runs over, the one named last changes fastest.
Arguments:
- grads: bfloat16 [8, 64, 1, 256, 6144], P('outer', 'dp'), may hold values from -0.4375 to 0.4375
- basis: bfloat16 [256, 6144], P(None, 'dp'), may hold values from -6 to 6
- weights: float32 [1, 256, 6144], P(None, 'dp'), may hold values from -10 to 10
- moment: float32 [1, 256, 6144], P(None, 'dp'), may hold values from -4 to 4
- second: float32 [1, 256, 6144], P(None, 'dp'), may hold values from 0.0001 to 0.01
Outputs:
- weight_new: float32 [1, 256, 6144], P(None, 'dp')
- moment_new: float32 [1, 256, 6144], P(None, 'dp')
- second_new: float32 [1, 256, 6144], P(None, 'dp')
- gathered: bfloat16 [1, 256, 6144], replicated
The draws below stay inside these ranges and needn't reach their ends.
All inputs are finite; a program needn't handle non-finite values.
Results may differ from the reference program's by a relative error of at most 0.006.
Values may be sent and summed in bfloat16 or wider, within the bound.
No kernel may reach another device: no remote copies, remote signals or barrier semaphores. Data moves between devices by JAX's collectives and lax.ppermute only.
A program may use at most 64 MiB of HBM per device.

```python
import math
import jax
import jax.numpy as jnp
from jax import lax

D = 6144
K = 256
LAYERS = 1
ROWS = 256
N_OUTER = 8
N_DP = 64


def draw_weights(key, part):
    key = jax.random.fold_in(key, 7)
    base_key, layer_key = jax.random.split(key)
    position = jnp.arange(ROWS, dtype=jnp.float32) / (ROWS - 1)
    base = jnp.clip(jax.random.normal(base_key, (LAYERS, ROWS, D), jnp.float32), -4.0, 4.0)
    row_scale = 0.5 * 3.0 ** position
    layer_scale = jnp.exp(jax.random.uniform(layer_key, (LAYERS, 1, 1), jnp.float32, -0.35, 0.33))
    return (base * row_scale[None, :, None] * layer_scale).astype(jnp.float32)


def strengthened(values, stream_key, source, target, shards_of, factor):
    owner, partner = [(jnp.arange(values.shape[axis_at]) // (values.shape[axis_at] // shards_of)).reshape([-1 if axis == axis_at else 1 for axis in range(values.ndim)]) for axis_at in (source, target)]
    chosen = jax.random.permutation(stream_key, shards_of)[partner]
    strong = (owner == chosen) | (owner == (partner + shards_of // 2) % shards_of)
    return jnp.where(strong, factor * values, values)


def block_levels(key, extent, pieces, smallest, high):
    factor_of, own = 1.0, jax.random.fold_in(key, 6)
    for dim, shards_of in pieces:
        steps = jnp.exp(jax.random.uniform(jax.random.fold_in(own, dim), (shards_of,), jnp.float32, smallest / len(pieces), high / len(pieces)))
        factor_of = factor_of * jnp.repeat(steps, extent[dim] // shards_of).reshape([-1 if axis == dim else 1 for axis in range(len(extent))])
    return factor_of


def bell_draw(own_key, extent, spread, reach, shards=(), kind=jnp.bfloat16):
    array = spread * jax.random.normal(own_key, extent, jnp.float32)
    if shards:
        array = array * block_levels(own_key, extent, shards, -0.22, 0.18)
    return jnp.clip(array, -reach, reach).astype(kind)


def heavy_noise(own_key, dims, spread, reach, cuts, heavy, kind=jnp.bfloat16):
    array = spread * jax.random.normal(own_key, dims, jnp.float32)
    if cuts:
        array = array * block_levels(own_key, dims, cuts, -0.22, 0.18)
    return jnp.clip(strengthened(array, jax.random.fold_in(own_key, 3), *heavy), -reach, reach).astype(kind)


def setup_inputs(seed: int = 0) -> dict:
    arg_keys = jax.random.split(jax.random.key(seed), 6)
    return {
        "grads": heavy_noise(arg_keys[0], (N_OUTER, N_DP, LAYERS, ROWS, D), 0.01, 0.4375, ((0, 8), (1, 64)), (1, 3, 64, 4.0)),
        "basis": bell_draw(arg_keys[1], (K, D), 1.0, 6.0, ((1, 64),)),
        "weights": draw_weights(jax.random.fold_in(arg_keys[5], 71), 0),
        "moment": bell_draw(arg_keys[3], (LAYERS, ROWS, D), 0.3, 4.0, ((1, 64),), jnp.float32),
        "second": jnp.clip(jnp.exp(math.log(0.01) - 4.6051702 * jax.random.uniform(arg_keys[4], (LAYERS, ROWS, D), jnp.float32) ** block_levels(arg_keys[4], (LAYERS, ROWS, D), ((1, 64),), -0.2, 0.2)), 0.0001, 0.01),
    }


beta_one = 0.9
beta_two = 0.999
bias_one = 1.0 - 0.9 ** 10
bias_two = 1.0 - 0.999 ** 10
adam_eps = 1e-06
norm_eps = 1e-06
decay = 0.01
rate = 0.1

def reference(grads, basis, weights, moment, second):
    replicas = grads.reshape(N_OUTER * N_DP, LAYERS * ROWS, D)

    def add_term(running, local_grad):
        term = jnp.dot(local_grad, basis.T, preferred_element_type=jnp.float32)
        return (running + term, None)
    sketch, _ = lax.scan(add_term, jnp.zeros((LAYERS * ROWS, K), jnp.float32), replicas)
    estimate = jnp.dot(sketch, basis.astype(jnp.float32), precision=lax.Precision.HIGHEST) / K
    estimate = estimate.reshape(LAYERS, ROWS, D)
    moment_new = beta_one * moment + (1.0 - beta_one) * estimate
    second_new = beta_two * second + (1.0 - beta_two) * estimate * estimate
    update = moment_new / bias_one / (jnp.sqrt(second_new / bias_two) + adam_eps) + decay * weights
    weight_sq = lax.optimization_barrier(jnp.sum(weights * weights, axis=(1, 2)))
    update_sq = lax.optimization_barrier(jnp.sum(update * update, axis=(1, 2)))
    trust_ratio = jnp.sqrt(weight_sq) / (jnp.sqrt(update_sq) + norm_eps)
    weight_new = weights - rate * trust_ratio[:, None, None] * update
    return (weight_new, moment_new, second_new, weight_new.astype(jnp.bfloat16))
```

```python
import jax
import jax.numpy as jnp
from jax import lax
from jax.sharding import Mesh
from jax.sharding import PartitionSpec as P

beta_one = 0.9
beta_two = 0.999
bias_one = 1.0 - 0.9**10
bias_two = 1.0 - 0.999**10
adam_eps = 1e-06
norm_eps = 1e-06
decay = 0.01
rate = 0.1

FINE = {"yh": 2, "x": 4, "yl": 2, "z": 16, "c": 2}
OUTER = ("yh", "x")
DP = ("yl", "z", "c")
PLANE = ("yl", "yh", "x")
SWAP = [(0, 1), (1, 0)]


def exchange(blocks, axes):
    return lax.all_to_all(blocks, axes, 0, 0, tiled=True)


def share(block, axes, count):
    return exchange(jnp.broadcast_to(block[None], (count,) + block.shape), axes)


def swap(block):
    return lax.ppermute(block, "c", SWAP)


def in_core_order(core, mine, other, axis):
    first = jnp.where(core == 0, mine, other)
    second = jnp.where(core == 0, other, mine)
    return first, second


def pieces(values, count):
    parts = []
    rest = values
    for _ in range(count):
        part = lax.reduce_precision(rest, 8, 7)
        parts.append(part.astype(jnp.bfloat16))
        rest = rest - part
    return jnp.concatenate(parts, axis=0)


def estimate_rows(halves, core, own_basis, other_basis, count):
    rows = halves.shape[1]
    total = 0.0
    for half, basis in ((core, own_basis), (1 - core, other_basis)):
        left = pieces(lax.dynamic_index_in_dim(halves, half, 0, keepdims=False), count)
        total = total + lax.dot_general(
            left, basis, (((1,), (1,)), ((), ())), preferred_element_type=jnp.float32
        )
    total = total.reshape(count, rows, -1)
    return jnp.sum(total, axis=0) / 256


def moments(estimate, weights, moment, second):
    moment_new = beta_one * moment + (1.0 - beta_one) * estimate
    second_new = beta_two * second + (1.0 - beta_two) * estimate * estimate
    update = moment_new / bias_one / (jnp.sqrt(second_new / bias_two) + adam_eps) + decay * weights
    return moment_new, second_new, update


def on_device(grads, basis, weights, moment, second):
    grad = grads[0, 0, 0]
    width = grad.shape[1]
    core = lax.axis_index("c")
    deep = lax.axis_index("z")
    low = lax.axis_index("yl")
    outer = lax.axis_index("yh") * 4 + lax.axis_index("x")

    state = jnp.concatenate([moment, second, weights], axis=0).astype(jnp.bfloat16)
    state_z = lax.all_gather(state, "z")
    other_grad = swap(grad)

    turned = basis.T
    half = turned.shape[1] // 2
    mine = lax.dynamic_slice_in_dim(turned, half * core, half, 1)
    theirs = swap(lax.dynamic_slice_in_dim(turned, half * (1 - core), half, 1))
    chip = jnp.concatenate(in_core_order(core, mine, theirs, 0), axis=0)
    part = chip.shape[0] // 8
    piece = lax.dynamic_slice_in_dim(chip, part * outer, part, 0)
    along_z = share(piece, "z", 16)
    blocks = share(along_z, PLANE, 16).reshape(2, 8, 16, part, half)
    own_basis = blocks.transpose(0, 2, 1, 3, 4).reshape(width, half)
    other_basis = swap(own_basis)

    contract = (((1,), (0,)), ((), ()))
    sketch = lax.dot_general(grad, own_basis, contract, preferred_element_type=jnp.float32)
    sketch = sketch + lax.dot_general(
        other_grad, own_basis, contract, preferred_element_type=jnp.float32
    )
    plane_sum = jnp.sum(exchange(sketch.reshape(16, 16, half), PLANE), axis=0)
    spread = jnp.broadcast_to(plane_sum.reshape(1, 2, 8, half), (16, 2, 8, half))
    halves = jnp.sum(
        exchange(spread.reshape(32, 8, half), ("z", "c")).reshape(16, 2, 8, half), axis=0
    )

    picked = lax.dynamic_index_in_dim(state_z, 2 * outer + core, 0, keepdims=False)
    passed = swap(lax.dynamic_index_in_dim(state_z, 2 * outer + 1 - core, 0, keepdims=False))
    m8, v8, w8 = jnp.concatenate(in_core_order(core, picked, passed, 1), axis=1).astype(jnp.float32)
    estimate8 = estimate_rows(halves, core, own_basis, other_basis, 2)
    _, _, update8 = moments(estimate8, w8, m8, v8)
    squares = jnp.stack([jnp.sum(w8 * w8), jnp.sum(update8 * update8)])
    notes = jnp.zeros((8, half), jnp.float32).at[0, :2].set(squares)
    for_core = halves.reshape(2, 2, 4, half).transpose(1, 0, 2, 3).reshape(2, 8, half)
    message = jnp.concatenate([for_core, jnp.broadcast_to(notes[None], (2, 8, half))], axis=1)
    inbox = exchange(
        jnp.broadcast_to(message[None], (16, 2, 16, half)).reshape(32, 16, half), PLANE + ("c",)
    )
    totals = jnp.sum(inbox[:, 8, :2], axis=0)
    trust_ratio = jnp.sqrt(totals[0]) / (jnp.sqrt(totals[1]) + norm_eps)
    rows8 = (w8 - rate * trust_ratio * update8).astype(jnp.bfloat16)
    rows_mine = share(rows8, PLANE, 16)
    rows_other = swap(rows_mine)
    gathered = jnp.stack(in_core_order(core, rows_mine, rows_other, 1), axis=1)
    gathered = gathered.reshape(1, 256, width)

    own = lax.dynamic_index_in_dim(inbox, low * 16 + deep, 0, keepdims=False)[:8]
    estimate = estimate_rows(own.reshape(2, 4, half), core, own_basis, other_basis, 3)[None]
    moment_new, second_new, update = moments(estimate, weights, moment, second)
    weight_new = weights - rate * trust_ratio * update
    return (weight_new, moment_new, second_new, gathered)


def solution(mesh):
    fine = Mesh(mesh.devices.reshape(tuple(FINE.values())), tuple(FINE))
    rows = P(None, DP, None)
    return jax.shard_map(
        on_device,
        mesh=fine,
        in_specs=(P(OUTER, DP, None, None, None), P(None, DP), rows, rows, rows),
        out_specs=(rows, rows, rows, P()),
        check_vma=False,
    )
```

```python
import jax
import jax.numpy as jnp
from jax import lax
from jax.experimental import pallas as pl
from jax.experimental.pallas import tpu as pltpu
from jax.sharding import Mesh
from jax.sharding import PartitionSpec as P

beta_one = 0.9
beta_two = 0.999
bias_one = 1.0 - 0.9**10
bias_two = 1.0 - 0.999**10
adam_eps = 1e-06
norm_eps = 1e-06
decay = 0.01
rate = 0.1

FINE = {"yh": 2, "x": 4, "yl": 2, "z": 16, "c": 2}
OUTER = ("yh", "x")
DP = ("yl", "z", "c")
PLANE = ("yl", "yh", "x")
SWAP = [(0, 1), (1, 0)]


def exchange(blocks, axes):
    return lax.all_to_all(blocks, axes, 0, 0, tiled=True)


def share(block, axes, count):
    return exchange(jnp.broadcast_to(block[None], (count,) + block.shape), axes)


def swap(block):
    return lax.ppermute(block, "c", SWAP)


def in_order(position, mine, other, axis):
    shape = [1] * (mine.ndim + 1)
    shape[axis] = 2
    here = (jnp.arange(2) == position).reshape(shape)
    return jnp.where(here, jnp.expand_dims(mine, axis), jnp.expand_dims(other, axis))


def pieces(values, count):
    parts = []
    rest = values
    for _ in range(count):
        part = lax.reduce_precision(rest, 8, 7)
        parts.append(part.astype(jnp.bfloat16))
        rest = rest - part
    return jnp.concatenate(parts, axis=0)


def estimate_rows(halves, core, own_basis, other_basis, count):
    rows = halves.shape[1]
    total = 0.0
    for half, basis in ((core, own_basis), (1 - core, other_basis)):
        left = pieces(lax.dynamic_index_in_dim(halves, half, 0, keepdims=False), count)
        total = total + lax.dot_general(
            left, basis, (((1,), (1,)), ((), ())), preferred_element_type=jnp.float32
        )
    total = total.reshape(count, rows, -1)
    return jnp.sum(total, axis=0) / 256


def moments(estimate, weights, moment, second):
    moment_new = beta_one * moment + (1.0 - beta_one) * estimate
    second_new = beta_two * second + (1.0 - beta_two) * estimate * estimate
    update = moment_new / bias_one / (jnp.sqrt(second_new / bias_two) + adam_eps) + decay * weights
    return moment_new, second_new, update


VMEM = pl.BlockSpec(memory_space=pltpu.VMEM)
SMEM = pl.BlockSpec(memory_space=pltpu.SMEM)
LIMIT = pltpu.CompilerParams(vmem_limit_bytes=40 << 20)
CHUNK = 512


def update_kernel(core_ref, terms_ref, own_ref, other_ref, state_ref, update_ref, message_ref):
    first, second = terms_ref[0], terms_ref[16]
    for step in range(1, 16):
        first = first + terms_ref[step]
        second = second + terms_ref[16 + step]
    at_first = core_ref[0] == 0

    def left_of(half):
        high = half.astype(jnp.bfloat16).astype(jnp.float32)
        return jnp.concatenate([high, half - high], axis=0).astype(jnp.bfloat16)

    left_own = left_of(jnp.where(at_first, first, second))
    left_other = left_of(jnp.where(at_first, second, first))
    contract = (((1,), (1,)), ((), ()))
    weight_sq = jnp.zeros((8, CHUNK), jnp.float32)
    update_sq = jnp.zeros((8, CHUNK), jnp.float32)
    for start in range(0, own_ref.shape[0], CHUNK):
        part = pl.ds(start, CHUNK)
        both = lax.dot_general(
            left_own, own_ref[part, :], contract, preferred_element_type=jnp.float32
        ) + lax.dot_general(
            left_other, other_ref[part, :], contract, preferred_element_type=jnp.float32
        )
        weights = state_ref[2, :, part]
        _, _, update = moments(
            (both[:8] + both[8:]) / 256, weights, state_ref[0, :, part], state_ref[1, :, part]
        )
        update_ref[:, part] = update
        weight_sq = weight_sq + weights * weights
        update_sq = update_sq + update * update
    row = lax.broadcasted_iota(jnp.int32, (8, 128), 0)
    lane = lax.broadcasted_iota(jnp.int32, (8, 128), 1)
    notes = jnp.where(
        (row == 0) & (lane == 0),
        jnp.sum(weight_sq),
        jnp.where((row == 0) & (lane == 1), jnp.sum(update_sq), 0.0),
    )
    for core in range(2):
        rows = slice(4 * core, 4 * core + 4)
        sent = jnp.concatenate([first[rows], second[rows]], axis=0)
        for place in range(16):
            message_ref[16 * core + place, 0:8, :] = sent
            message_ref[16 * core + place, 8:16, :] = notes


def rows_kernel(inbox_ref, update_ref, state_ref, rows_ref, ratio_ref):
    notes = inbox_ref[0, 8:16, :]
    for source in range(1, 32):
        notes = notes + inbox_ref[source, 8:16, :]
    lane = lax.broadcasted_iota(jnp.int32, (8, 128), 1)
    weight_sq = jnp.sum(jnp.where(lane == 0, notes, 0.0), keepdims=True)
    update_sq = jnp.sum(jnp.where(lane == 1, notes, 0.0), keepdims=True)
    ratio = jnp.sqrt(weight_sq) / (jnp.sqrt(update_sq) + norm_eps)
    ratio_ref[...] = jnp.broadcast_to(ratio, (8, 128))
    for start in range(0, update_ref.shape[1], CHUNK):
        part = pl.ds(start, CHUNK)
        rows = (state_ref[2, :, part] - rate * ratio * update_ref[:, part]).astype(jnp.bfloat16)
        for place in range(16):
            rows_ref[place, :, part] = rows


def order_kernel(core_ref, mine_ref, other_ref, out_ref):
    mine = mine_ref[0].astype(jnp.float32)
    other = other_ref[0].astype(jnp.float32)
    at_first = core_ref[0] == 0
    both = [jnp.where(at_first, mine, other), jnp.where(at_first, other, mine)]
    out_ref[...] = jnp.concatenate(both, axis=0).astype(jnp.bfloat16)


def on_device(grads, basis, weights, moment, second):
    grad = grads[0, 0, 0]
    width = grad.shape[1]
    core = lax.axis_index("c")
    deep = lax.axis_index("z")
    low = lax.axis_index("yl")
    outer = lax.axis_index("yh") * 4 + lax.axis_index("x")
    core_at = core.astype(jnp.int32).reshape(1)

    turned = basis.T
    half = turned.shape[1] // 2
    mine = lax.dynamic_slice_in_dim(turned, half * core, half, 1)
    theirs = swap(lax.dynamic_slice_in_dim(turned, half * (1 - core), half, 1))
    chip = in_order(core, mine, theirs, 0).reshape(-1, half)
    part = chip.shape[0] // 8
    piece = lax.dynamic_slice_in_dim(chip, part * outer, part, 0)
    state = jnp.concatenate([moment, second, weights], axis=0).astype(jnp.bfloat16)
    state_z = lax.all_gather(state, "z")
    along_z = share(piece, "z", 16)
    other_grad = swap(grad)
    blocks = share(along_z, PLANE, 16).reshape(2, 8, 16, part, half)
    own_basis = blocks.transpose(0, 2, 1, 3, 4).reshape(width, half)
    other_basis = swap(own_basis)

    contract = (((1,), (0,)), ((), ()))
    sketch = lax.dot_general(grad, own_basis, contract, preferred_element_type=jnp.float32)
    sketch = sketch + lax.dot_general(
        other_grad, own_basis, contract, preferred_element_type=jnp.float32
    )
    plane_terms = exchange(sketch.reshape(16, 16, half), PLANE)
    plane_terms, state_z = lax.optimization_barrier((plane_terms, state_z))
    plane_sum = jnp.sum(plane_terms, axis=0)
    spread = jnp.broadcast_to(plane_sum.reshape(2, 1, 8, half), (2, 16, 8, half))
    terms = exchange(spread.reshape(32, 8, half), ("c", "z"))

    picked = lax.dynamic_index_in_dim(state_z, 2 * outer + core, 0, keepdims=False)
    passed = swap(lax.dynamic_index_in_dim(state_z, 2 * outer + 1 - core, 0, keepdims=False))
    state8 = in_order(core, picked, passed, 1).reshape(3, 8, width).astype(jnp.float32)
    update8, message = pl.pallas_call(
        update_kernel,
        out_shape=(
            jax.ShapeDtypeStruct((8, width), jnp.float32),
            jax.ShapeDtypeStruct((32, 16, half), jnp.float32),
        ),
        in_specs=[SMEM, VMEM, VMEM, VMEM, VMEM],
        out_specs=(VMEM, VMEM),
        compiler_params=LIMIT,
        name="update",
    )(core_at, terms, own_basis, other_basis, state8)
    inbox = exchange(message, ("c",) + PLANE)
    rows_out, ratio = pl.pallas_call(
        rows_kernel,
        out_shape=(
            jax.ShapeDtypeStruct((16, 8, width), jnp.bfloat16),
            jax.ShapeDtypeStruct((8, 128), jnp.float32),
        ),
        in_specs=[VMEM, VMEM, VMEM],
        out_specs=(VMEM, VMEM),
        compiler_params=LIMIT,
        name="rows",
    )(inbox, update8, state8)
    rows_mine = exchange(rows_out, PLANE)
    rows_other = swap(rows_mine)
    gathered = pl.pallas_call(
        order_kernel,
        grid=(16,),
        out_shape=jax.ShapeDtypeStruct((256, width), jnp.bfloat16),
        in_specs=[
            SMEM,
            pl.BlockSpec((1, 8, width), lambda i: (i, 0, 0)),
            pl.BlockSpec((1, 8, width), lambda i: (i, 0, 0)),
        ],
        out_specs=pl.BlockSpec((16, width), lambda i: (i, 0)),
        name="order",
    )(core_at, rows_mine, rows_other)[None]

    trust_ratio = ratio[0, 0]
    source = (deep % 2) * 16 + low * 8 + deep // 2
    own = lax.dynamic_index_in_dim(inbox, source, 0, keepdims=False)[:8]
    estimate = estimate_rows(own.reshape(2, 4, half), core, own_basis, other_basis, 3)[None]
    moment_new, second_new, update = moments(estimate, weights, moment, second)
    weight_new = weights - rate * trust_ratio * update
    return (weight_new, moment_new, second_new, gathered)


def solution(mesh):
    fine = Mesh(mesh.devices.reshape(tuple(FINE.values())), tuple(FINE))
    rows = P(None, DP, None)
    return jax.shard_map(
        on_device,
        mesh=fine,
        in_specs=(P(OUTER, DP, None, None, None), P(None, DP), rows, rows, rows),
        out_specs=(rows, rows, rows, P()),
        check_vma=False,
    )
```

```python
import jax
import jax.numpy as jnp
from jax import lax
from jax.experimental import pallas as pl
from jax.experimental.pallas import tpu as pltpu
from jax.sharding import Mesh
from jax.sharding import PartitionSpec as P

beta_one = 0.9
beta_two = 0.999
bias_one = 1.0 - 0.9**10
bias_two = 1.0 - 0.999**10
adam_eps = 1e-06
norm_eps = 1e-06
decay = 0.01
rate = 0.1

FINE = {"yh": 2, "x": 4, "yl": 2, "z": 16, "c": 2}
OUTER = ("yh", "x")
DP = ("yl", "z", "c")
PLANE = ("yl", "yh", "x")
SWAP = [(0, 1), (1, 0)]
ALL = tuple(FINE)


def flat(outer, low, deep, core):
    return ((outer * 2 + low) * 16 + deep) * 2 + core


def state_moves(other):
    return [
        (flat(o, low, z, c), flat(z // 2, low, 2 * o + (1 - c if other else c), z % 2))
        for o in range(8)
        for low in range(2)
        for z in range(16)
        for c in range(2)
    ]


def exchange(blocks, axes):
    return lax.all_to_all(blocks, axes, 0, 0, tiled=True)


def share(block, axes, count):
    return exchange(jnp.broadcast_to(block[None], (count,) + block.shape), axes)


def swap(block):
    return lax.ppermute(block, "c", SWAP)


def in_order(position, mine, other, axis):
    shape = [1] * (mine.ndim + 1)
    shape[axis] = 2
    here = (jnp.arange(2) == position).reshape(shape)
    return jnp.where(here, jnp.expand_dims(mine, axis), jnp.expand_dims(other, axis))


def pieces(values, count):
    parts = []
    rest = values
    for _ in range(count):
        part = lax.reduce_precision(rest, 8, 7)
        parts.append(part.astype(jnp.bfloat16))
        rest = rest - part
    return jnp.concatenate(parts, axis=0)


def estimate_rows(halves, core, own_basis, other_basis, count):
    rows = halves.shape[1]
    total = 0.0
    for half, basis in ((core, own_basis), (1 - core, other_basis)):
        left = pieces(lax.dynamic_index_in_dim(halves, half, 0, keepdims=False), count)
        total = total + lax.dot_general(
            left, basis, (((1,), (1,)), ((), ())), preferred_element_type=jnp.float32
        )
    total = total.reshape(count, rows, -1)
    return jnp.sum(total, axis=0) / 256


def moments(estimate, weights, moment, second):
    moment_new = beta_one * moment + (1.0 - beta_one) * estimate
    second_new = beta_two * second + (1.0 - beta_two) * estimate * estimate
    update = moment_new / bias_one / (jnp.sqrt(second_new / bias_two) + adam_eps) + decay * weights
    return moment_new, second_new, update


VMEM = pl.BlockSpec(memory_space=pltpu.VMEM)
SMEM = pl.BlockSpec(memory_space=pltpu.SMEM)
LIMIT = pltpu.CompilerParams(vmem_limit_bytes=40 << 20)
CHUNK = 512


def update_kernel(core_ref, terms_ref, own_ref, other_ref, state_ref, update_ref, message_ref):
    first, second = terms_ref[0], terms_ref[16]
    for step in range(1, 16):
        first = first + terms_ref[step]
        second = second + terms_ref[16 + step]
    at_first = core_ref[0] == 0

    def left_of(half):
        high = half.astype(jnp.bfloat16).astype(jnp.float32)
        return jnp.concatenate([high, half - high], axis=0).astype(jnp.bfloat16)

    left_own = left_of(jnp.where(at_first, first, second))
    left_other = left_of(jnp.where(at_first, second, first))
    contract = (((1,), (1,)), ((), ()))
    weight_sq = jnp.zeros((8, CHUNK), jnp.float32)
    update_sq = jnp.zeros((8, CHUNK), jnp.float32)
    for start in range(0, own_ref.shape[0], CHUNK):
        part = pl.ds(start, CHUNK)
        both = lax.dot_general(
            left_own, own_ref[part, :], contract, preferred_element_type=jnp.float32
        ) + lax.dot_general(
            left_other, other_ref[part, :], contract, preferred_element_type=jnp.float32
        )
        weights = state_ref[2, :, part]
        _, _, update = moments(
            (both[:8] + both[8:]) / 256, weights, state_ref[0, :, part], state_ref[1, :, part]
        )
        update_ref[:, part] = update
        weight_sq = weight_sq + weights * weights
        update_sq = update_sq + update * update
    row = lax.broadcasted_iota(jnp.int32, (8, 128), 0)
    lane = lax.broadcasted_iota(jnp.int32, (8, 128), 1)
    notes = jnp.where(
        (row == 0) & (lane == 0),
        jnp.sum(weight_sq),
        jnp.where((row == 0) & (lane == 1), jnp.sum(update_sq), 0.0),
    )
    for core in range(2):
        rows = slice(4 * core, 4 * core + 4)
        sent = jnp.concatenate([first[rows], second[rows]], axis=0)
        for place in range(16):
            message_ref[2 * place + core, 0:8, :] = sent
            message_ref[2 * place + core, 8:16, :] = notes


def rows_kernel(inbox_ref, update_ref, state_ref, rows_ref, ratio_ref):
    notes = inbox_ref[0, 8:16, :]
    for source in range(1, 32):
        notes = notes + inbox_ref[source, 8:16, :]
    lane = lax.broadcasted_iota(jnp.int32, (8, 128), 1)
    weight_sq = jnp.sum(jnp.where(lane == 0, notes, 0.0), keepdims=True)
    update_sq = jnp.sum(jnp.where(lane == 1, notes, 0.0), keepdims=True)
    ratio = jnp.sqrt(weight_sq) / (jnp.sqrt(update_sq) + norm_eps)
    ratio_ref[...] = jnp.broadcast_to(ratio, (8, 128))
    for start in range(0, update_ref.shape[1], CHUNK):
        part = pl.ds(start, CHUNK)
        rows = (state_ref[2, :, part] - rate * ratio * update_ref[:, part]).astype(jnp.bfloat16)
        for place in range(16):
            rows_ref[place, :, part] = rows


def place_kernel(at_ref, rows_ref, *refs):
    out_ref, sems = refs[-2:]
    copies = [
        pltpu.make_async_copy(rows_ref.at[i], out_ref.at[i, at_ref[0]], sems.at[i])
        for i in range(16)
    ]
    for copy in copies:
        copy.start()
    for copy in copies:
        copy.wait()


def place(at, rows, *partly):
    shape = (16, 2) + rows.shape[1:]
    return pl.pallas_call(
        place_kernel,
        out_shape=jax.ShapeDtypeStruct(shape, rows.dtype),
        in_specs=[SMEM, VMEM] + [pl.BlockSpec(memory_space=pl.ANY)] * len(partly),
        out_specs=pl.BlockSpec(memory_space=pl.ANY),
        scratch_shapes=[pltpu.SemaphoreType.DMA((16,))],
        input_output_aliases={2: 0} if partly else {},
        name="place",
    )(at, rows, *partly)


def on_device(grads, basis, weights, moment, second):
    grad = grads[0, 0, 0]
    width = grad.shape[1]
    core = lax.axis_index("c")
    deep = lax.axis_index("z")
    low = lax.axis_index("yl")
    outer = lax.axis_index("yh") * 4 + lax.axis_index("x")
    core_at = core.astype(jnp.int32).reshape(1)

    turned = basis.T
    half = turned.shape[1] // 2
    mine = lax.dynamic_slice_in_dim(turned, half * core, half, 1)
    theirs = swap(lax.dynamic_slice_in_dim(turned, half * (1 - core), half, 1))
    chip = in_order(core, mine, theirs, 0).reshape(-1, half)
    part = chip.shape[0] // 8
    piece = lax.dynamic_slice_in_dim(chip, part * outer, part, 0)
    along_z = share(piece, "z", 16)
    other_grad = swap(grad)
    blocks = share(along_z, PLANE, 16).reshape(2, 8, 16, part, half)
    own_basis = blocks.transpose(0, 2, 1, 3, 4).reshape(width, half)
    other_basis = swap(own_basis)

    contract = (((1,), (0,)), ((), ()))
    sketch = lax.dot_general(grad, own_basis, contract, preferred_element_type=jnp.float32)
    sketch = sketch + lax.dot_general(
        other_grad, own_basis, contract, preferred_element_type=jnp.float32
    )
    sketch, m_in, v_in, w_in = lax.optimization_barrier((sketch, moment, second, weights))
    plane_terms = exchange(sketch.reshape(16, 16, half), PLANE)
    plane_sum = jnp.sum(plane_terms, axis=0)
    spread = jnp.broadcast_to(plane_sum.reshape(2, 1, 8, half), (2, 16, 8, half))
    terms = exchange(spread.reshape(32, 8, half), ("c", "z"))

    state = jnp.stack([m_in[0], v_in[0], w_in[0]]).astype(jnp.bfloat16)
    state_one = lax.ppermute(state, ALL, state_moves(False))
    state_two = lax.ppermute(state, ALL, state_moves(True))
    state8 = in_order(deep % 2, state_one, state_two, 1).reshape(3, 8, width).astype(jnp.float32)
    update8, message = pl.pallas_call(
        update_kernel,
        out_shape=(
            jax.ShapeDtypeStruct((8, width), jnp.float32),
            jax.ShapeDtypeStruct((32, 16, half), jnp.float32),
        ),
        in_specs=[SMEM, VMEM, VMEM, VMEM, VMEM],
        out_specs=(VMEM, VMEM),
        compiler_params=LIMIT,
        name="update",
    )(core_at, terms, own_basis, other_basis, state8)
    inbox = exchange(message, PLANE + ("c",))
    rows_out, ratio = pl.pallas_call(
        rows_kernel,
        out_shape=(
            jax.ShapeDtypeStruct((16, 8, width), jnp.bfloat16),
            jax.ShapeDtypeStruct((8, 128), jnp.float32),
        ),
        in_specs=[VMEM, VMEM, VMEM],
        out_specs=(VMEM, VMEM),
        compiler_params=LIMIT,
        name="rows",
    )(inbox, update8, state8)
    rows_mine = exchange(rows_out, PLANE)
    rows_other = swap(rows_mine)
    gathered = place(1 - core_at, rows_other, place(core_at, rows_mine))
    gathered = gathered.reshape(1, 256, width)

    trust_ratio = ratio[0, 0]
    own = lax.dynamic_index_in_dim(inbox, low * 16 + deep, 0, keepdims=False)[:8]
    estimate = estimate_rows(own.reshape(2, 4, half), core, own_basis, other_basis, 3)[None]
    moment_new, second_new, update = moments(estimate, weights, moment, second)
    weight_new = weights - rate * trust_ratio * update
    return (weight_new, moment_new, second_new, gathered)


def solution(mesh):
    fine = Mesh(mesh.devices.reshape(tuple(FINE.values())), tuple(FINE))
    rows = P(None, DP, None)
    return jax.shard_map(
        on_device,
        mesh=fine,
        in_specs=(P(OUTER, DP, None, None, None), P(None, DP), rows, rows, rows),
        out_specs=(rows, rows, rows, P()),
        check_vma=False,
    )
```

```python
import jax
import jax.numpy as jnp
from jax import lax
from jax.experimental import pallas as pl
from jax.experimental.pallas import tpu as pltpu
from jax.sharding import Mesh
from jax.sharding import PartitionSpec as P

beta_one = 0.9
beta_two = 0.999
bias_one = 1.0 - 0.9**10
bias_two = 1.0 - 0.999**10
adam_eps = 1e-06
norm_eps = 1e-06
decay = 0.01
rate = 0.1

FINE = {"yh": 2, "x": 4, "yl": 2, "z": 16, "c": 2}
OUTER = ("yh", "x")
DP = ("yl", "z", "c")
PLANE = ("yl", "yh", "x")
SWAP = [(0, 1), (1, 0)]
ALL = tuple(FINE)


def flat(outer, low, deep, core):
    return ((outer * 2 + low) * 16 + deep) * 2 + core


def state_moves(other):
    return [
        (flat(o, low, z, c), flat(z // 2, low, 2 * o + (1 - c if other else c), z % 2))
        for o in range(8)
        for low in range(2)
        for z in range(16)
        for c in range(2)
    ]


def exchange(blocks, axes):
    return lax.all_to_all(blocks, axes, 0, 0, tiled=True)


def share(block, axes, count):
    return exchange(jnp.broadcast_to(block[None], (count,) + block.shape), axes)


def swap(block):
    return lax.ppermute(block, "c", SWAP)


def in_order(position, mine, other, axis):
    shape = [1] * (mine.ndim + 1)
    shape[axis] = 2
    here = (jnp.arange(2) == position).reshape(shape)
    return jnp.where(here, jnp.expand_dims(mine, axis), jnp.expand_dims(other, axis))


def pieces(values, count):
    parts = []
    rest = values
    for _ in range(count):
        part = lax.reduce_precision(rest, 8, 7)
        parts.append(part.astype(jnp.bfloat16))
        rest = rest - part
    return jnp.concatenate(parts, axis=0)


def estimate_rows(halves, core, own_basis, other_basis, count):
    rows = halves.shape[1]
    total = 0.0
    for half, basis in ((core, own_basis), (1 - core, other_basis)):
        left = pieces(lax.dynamic_index_in_dim(halves, half, 0, keepdims=False), count)
        total = total + lax.dot_general(
            left, basis, (((1,), (1,)), ((), ())), preferred_element_type=jnp.float32
        )
    total = total.reshape(count, rows, -1)
    return jnp.sum(total, axis=0) / 256


def moments(estimate, weights, moment, second):
    moment_new = beta_one * moment + (1.0 - beta_one) * estimate
    second_new = beta_two * second + (1.0 - beta_two) * estimate * estimate
    update = moment_new / bias_one / (jnp.sqrt(second_new / bias_two) + adam_eps) + decay * weights
    return moment_new, second_new, update


VMEM = pl.BlockSpec(memory_space=pltpu.VMEM)
SMEM = pl.BlockSpec(memory_space=pltpu.SMEM)
LIMIT = pltpu.CompilerParams(vmem_limit_bytes=12 << 20)
CHUNK = 512


def pack_kernel(moment_ref, second_ref, weights_ref, out_ref):
    rows = [moment_ref[0], second_ref[0], weights_ref[0]]
    out_ref[...] = jnp.concatenate(rows, axis=0).astype(jnp.bfloat16)


def product_kernel(grad_ref, other_ref, basis_ref, out_ref):
    basis = basis_ref[...]
    total = jnp.dot(grad_ref[...], basis, preferred_element_type=jnp.float32)
    out_ref[...] = total + jnp.dot(other_ref[...], basis, preferred_element_type=jnp.float32)


def update_kernel(
    at_ref, terms_ref, own_ref, other_ref, one_ref, two_ref, update_ref, kept_ref, message_ref
):
    first, second = terms_ref[0], terms_ref[16]
    for step in range(1, 16):
        first = first + terms_ref[step]
        second = second + terms_ref[16 + step]
    at_first = at_ref[0] == 0
    one_first = at_ref[1] == 0

    def left_of(half):
        high = half.astype(jnp.bfloat16).astype(jnp.float32)
        return jnp.concatenate([high, half - high], axis=0).astype(jnp.bfloat16)

    left_own = left_of(jnp.where(at_first, first, second))
    left_other = left_of(jnp.where(at_first, second, first))
    contract = (((1,), (1,)), ((), ()))
    weight_sq = jnp.zeros((8, CHUNK), jnp.float32)
    update_sq = jnp.zeros((8, CHUNK), jnp.float32)
    for start in range(0, own_ref.shape[0], CHUNK):
        part = pl.ds(start, CHUNK)
        both = lax.dot_general(
            left_own, own_ref[part, :], contract, preferred_element_type=jnp.float32
        ) + lax.dot_general(
            left_other, other_ref[part, :], contract, preferred_element_type=jnp.float32
        )
        one = one_ref[:, part].astype(jnp.float32)
        two = two_ref[:, part].astype(jnp.float32)
        upper = jnp.where(one_first, one, two)
        lower = jnp.where(one_first, two, one)
        moment, before, weights = [
            jnp.concatenate([upper[r : r + 4], lower[r : r + 4]], axis=0) for r in (0, 4, 8)
        ]
        _, _, update = moments((both[:8] + both[8:]) / 256, weights, moment, before)
        update_ref[:, part] = update
        kept_ref[:, part] = weights
        weight_sq = weight_sq + weights * weights
        update_sq = update_sq + update * update
    row = lax.broadcasted_iota(jnp.int32, (8, 128), 0)
    lane = lax.broadcasted_iota(jnp.int32, (8, 128), 1)
    notes = jnp.where(
        (row == 0) & (lane == 0),
        jnp.sum(weight_sq),
        jnp.where((row == 0) & (lane == 1), jnp.sum(update_sq), 0.0),
    )
    for core in range(2):
        rows = slice(4 * core, 4 * core + 4)
        sent = jnp.concatenate([first[rows], second[rows]], axis=0)
        for place in range(16):
            message_ref[2 * place + core, 0:8, :] = sent
            message_ref[2 * place + core, 8:16, :] = notes


def rows_kernel(inbox_ref, update_ref, kept_ref, rows_ref, ratio_ref):
    notes = inbox_ref[0, 8:16, :]
    for source in range(1, 32):
        notes = notes + inbox_ref[source, 8:16, :]
    lane = lax.broadcasted_iota(jnp.int32, (8, 128), 1)
    weight_sq = jnp.sum(jnp.where(lane == 0, notes, 0.0), keepdims=True)
    update_sq = jnp.sum(jnp.where(lane == 1, notes, 0.0), keepdims=True)
    ratio = jnp.sqrt(weight_sq) / (jnp.sqrt(update_sq) + norm_eps)
    ratio_ref[...] = jnp.broadcast_to(ratio, (8, 128))
    for start in range(0, update_ref.shape[1], CHUNK):
        part = pl.ds(start, CHUNK)
        rows = (kept_ref[:, part] - rate * ratio * update_ref[:, part]).astype(jnp.bfloat16)
        for place in range(16):
            rows_ref[place, :, part] = rows


def place_kernel(at_ref, rows_ref, *refs):
    out_ref, sems = refs[-2:]
    copies = [
        pltpu.make_async_copy(rows_ref.at[i], out_ref.at[i, at_ref[0]], sems.at[i])
        for i in range(16)
    ]
    for copy in copies:
        copy.start()
    for copy in copies:
        copy.wait()


def place(at, rows, *partly):
    shape = (16, 2) + rows.shape[1:]
    return pl.pallas_call(
        place_kernel,
        out_shape=jax.ShapeDtypeStruct(shape, rows.dtype),
        in_specs=[SMEM] + [pl.BlockSpec(memory_space=pl.ANY)] * (1 + len(partly)),
        out_specs=pl.BlockSpec(memory_space=pl.ANY),
        scratch_shapes=[pltpu.SemaphoreType.DMA((16,))],
        input_output_aliases={2: 0} if partly else {},
        cost_estimate=pl.CostEstimate(flops=0, bytes_accessed=2 * rows.nbytes, transcendentals=0),
        name="place",
    )(at, rows, *partly)


def on_device(grads, basis, weights, moment, second):
    grad = grads[0, 0, 0]
    width = grad.shape[1]
    core = lax.axis_index("c")
    deep = lax.axis_index("z")
    low = lax.axis_index("yl")
    outer = lax.axis_index("yh") * 4 + lax.axis_index("x")
    core_at = core.astype(jnp.int32).reshape(1)

    turned = basis.T
    half = turned.shape[1] // 2
    mine = lax.dynamic_slice_in_dim(turned, half * core, half, 1)
    theirs = swap(lax.dynamic_slice_in_dim(turned, half * (1 - core), half, 1))
    chip = in_order(core, mine, theirs, 0).reshape(-1, half)
    part = chip.shape[0] // 8
    piece = lax.dynamic_slice_in_dim(chip, part * outer, part, 0)
    along_z = share(piece, "z", 16)
    along_z, m_in, v_in, w_in = lax.optimization_barrier((along_z, moment, second, weights))
    state = pl.pallas_call(
        pack_kernel,
        out_shape=jax.ShapeDtypeStruct((12, width), jnp.bfloat16),
        in_specs=[VMEM, VMEM, VMEM],
        out_specs=VMEM,
        name="pack",
    )(m_in, v_in, w_in)
    state_one = lax.ppermute(state, ALL, state_moves(False))
    state_two = lax.ppermute(state, ALL, state_moves(True))
    other_grad = swap(grad)
    blocks = share(along_z, PLANE, 16)
    blocks, state_one, state_two = lax.optimization_barrier((blocks, state_one, state_two))
    blocks = blocks.reshape(2, 8, 16, part, half)
    own_basis = blocks.transpose(0, 2, 1, 3, 4).reshape(width, half)

    sketch = pl.pallas_call(
        product_kernel,
        out_shape=jax.ShapeDtypeStruct((grad.shape[0], half), jnp.float32),
        in_specs=[VMEM, VMEM, VMEM],
        out_specs=VMEM,
        compiler_params=LIMIT,
        name="product",
    )(grad, other_grad, own_basis)
    sketch, basis_sent = lax.optimization_barrier((sketch, own_basis))
    other_basis = swap(basis_sent)
    plane_terms = exchange(sketch.reshape(16, 16, half), PLANE)
    plane_sum = jnp.sum(plane_terms, axis=0)
    spread = jnp.broadcast_to(plane_sum.reshape(2, 1, 8, half), (2, 16, 8, half))
    terms = exchange(spread.reshape(32, 8, half), ("c", "z"))

    wide = jax.ShapeDtypeStruct((8, width), jnp.float32)
    update8, kept8, message = pl.pallas_call(
        update_kernel,
        out_shape=(wide, wide, jax.ShapeDtypeStruct((32, 16, half), jnp.float32)),
        in_specs=[SMEM, VMEM, VMEM, VMEM, VMEM, VMEM],
        out_specs=(VMEM, VMEM, VMEM),
        compiler_params=LIMIT,
        name="update",
    )(
        jnp.stack([core, deep % 2]).astype(jnp.int32),
        terms,
        own_basis,
        other_basis,
        state_one,
        state_two,
    )
    inbox = exchange(message, PLANE + ("c",))
    rows_out, ratio = pl.pallas_call(
        rows_kernel,
        out_shape=(
            jax.ShapeDtypeStruct((16, 8, width), jnp.bfloat16),
            jax.ShapeDtypeStruct((8, 128), jnp.float32),
        ),
        in_specs=[VMEM, VMEM, VMEM],
        out_specs=(VMEM, VMEM),
        compiler_params=LIMIT,
        name="rows",
    )(inbox, update8, kept8)
    rows_mine = exchange(rows_out, PLANE)
    rows_other = swap(rows_mine)
    partly = place(core_at, rows_mine)
    partly, inbox, ratio = lax.optimization_barrier((partly, inbox, ratio))
    gathered = place(1 - core_at, rows_other, partly)
    gathered = gathered.reshape(1, 256, width)

    trust_ratio = ratio[0, 0]
    own = lax.dynamic_index_in_dim(inbox, low * 16 + deep, 0, keepdims=False)[:8]
    estimate = estimate_rows(own.reshape(2, 4, half), core, own_basis, other_basis, 3)[None]
    moment_new, second_new, update = moments(estimate, weights, moment, second)
    weight_new = weights - rate * trust_ratio * update
    return (weight_new, moment_new, second_new, gathered)


def solution(mesh):
    fine = Mesh(mesh.devices.reshape(tuple(FINE.values())), tuple(FINE))
    rows = P(None, DP, None)
    return jax.shard_map(
        on_device,
        mesh=fine,
        in_specs=(P(OUTER, DP, None, None, None), P(None, DP), rows, rows, rows),
        out_specs=(rows, rows, rows, P()),
        check_vma=False,
    )
```

```python
import jax
import jax.numpy as jnp
from jax import lax
from jax.experimental import pallas as pl
from jax.experimental.pallas import tpu as pltpu
from jax.sharding import Mesh
from jax.sharding import PartitionSpec as P

beta_one = 0.9
beta_two = 0.999
bias_one = 1.0 - 0.9**10
bias_two = 1.0 - 0.999**10
adam_eps = 1e-06
norm_eps = 1e-06
decay = 0.01
rate = 0.1

FINE = {"yh": 2, "x": 4, "yl": 2, "z": 16, "c": 2}
OUTER = ("yh", "x")
DP = ("yl", "z", "c")
PLANE = ("yl", "yh", "x")
SWAP = [(0, 1), (1, 0)]


def exchange(blocks, axes):
    return lax.all_to_all(blocks, axes, 0, 0, tiled=True)


def share(block, axes, count):
    return exchange(jnp.broadcast_to(block[None], (count,) + block.shape), axes)


def swap(block):
    return lax.ppermute(block, "c", SWAP)


def in_order(position, mine, other, axis):
    shape = [1] * (mine.ndim + 1)
    shape[axis] = 2
    here = (jnp.arange(2) == position).reshape(shape)
    return jnp.where(here, jnp.expand_dims(mine, axis), jnp.expand_dims(other, axis))


def pieces(values, count):
    parts = []
    rest = values
    for _ in range(count):
        part = lax.reduce_precision(rest, 8, 7)
        parts.append(part.astype(jnp.bfloat16))
        rest = rest - part
    return jnp.concatenate(parts, axis=0)


def estimate_rows(halves, core, own_basis, other_basis, count):
    rows = halves.shape[1]
    total = 0.0
    for half, basis in ((core, own_basis), (1 - core, other_basis)):
        left = pieces(lax.dynamic_index_in_dim(halves, half, 0, keepdims=False), count)
        total = total + lax.dot_general(
            left, basis, (((1,), (1,)), ((), ())), preferred_element_type=jnp.float32
        )
    total = total.reshape(count, rows, -1)
    return jnp.sum(total, axis=0) / 256


def moments(estimate, weights, moment, second):
    moment_new = beta_one * moment + (1.0 - beta_one) * estimate
    second_new = beta_two * second + (1.0 - beta_two) * estimate * estimate
    update = moment_new / bias_one / (jnp.sqrt(second_new / bias_two) + adam_eps) + decay * weights
    return moment_new, second_new, update


VMEM = pl.BlockSpec(memory_space=pltpu.VMEM)
SMEM = pl.BlockSpec(memory_space=pltpu.SMEM)
LIMIT = pltpu.CompilerParams(vmem_limit_bytes=12 << 20)
CHUNK = 512


def pack_kernel(moment_ref, second_ref, weights_ref, out_ref):
    rows = [moment_ref[0], second_ref[0], weights_ref[0]]
    out_ref[...] = jnp.concatenate(rows, axis=0).astype(jnp.bfloat16)


def product_kernel(grad_ref, other_ref, basis_ref, out_ref):
    basis = basis_ref[...]
    total = jnp.dot(grad_ref[...], basis, preferred_element_type=jnp.float32)
    out_ref[...] = total + jnp.dot(other_ref[...], basis, preferred_element_type=jnp.float32)


def update_kernel(
    at_ref, terms_ref, own_ref, other_ref, one_ref, two_ref, update_ref, kept_ref, message_ref
):
    first, second = terms_ref[0], terms_ref[16]
    for step in range(1, 16):
        first = first + terms_ref[step]
        second = second + terms_ref[16 + step]
    at_first = at_ref[0] == 0
    one_first = at_ref[1] == 0

    def left_of(half):
        high = half.astype(jnp.bfloat16).astype(jnp.float32)
        return jnp.concatenate([high, half - high], axis=0).astype(jnp.bfloat16)

    left_own = left_of(jnp.where(at_first, first, second))
    left_other = left_of(jnp.where(at_first, second, first))
    contract = (((1,), (1,)), ((), ()))
    weight_sq = jnp.zeros((8, CHUNK), jnp.float32)
    update_sq = jnp.zeros((8, CHUNK), jnp.float32)
    for start in range(0, own_ref.shape[0], CHUNK):
        part = pl.ds(start, CHUNK)
        both = lax.dot_general(
            left_own, own_ref[part, :], contract, preferred_element_type=jnp.float32
        ) + lax.dot_general(
            left_other, other_ref[part, :], contract, preferred_element_type=jnp.float32
        )
        one = one_ref[:, part].astype(jnp.float32)
        two = two_ref[:, part].astype(jnp.float32)
        upper = jnp.where(one_first, one, two)
        lower = jnp.where(one_first, two, one)
        moment, before, weights = [
            jnp.concatenate([upper[r : r + 4], lower[r : r + 4]], axis=0) for r in (0, 4, 8)
        ]
        _, _, update = moments((both[:8] + both[8:]) / 256, weights, moment, before)
        update_ref[:, part] = update
        kept_ref[:, part] = weights
        weight_sq = weight_sq + weights * weights
        update_sq = update_sq + update * update
    row = lax.broadcasted_iota(jnp.int32, (8, 128), 0)
    lane = lax.broadcasted_iota(jnp.int32, (8, 128), 1)
    notes = jnp.where(
        (row == 0) & (lane == 0),
        jnp.sum(weight_sq),
        jnp.where((row == 0) & (lane == 1), jnp.sum(update_sq), 0.0),
    )
    for core in range(2):
        rows = slice(4 * core, 4 * core + 4)
        sent = jnp.concatenate([first[rows], second[rows]], axis=0)
        for place in range(16):
            message_ref[2 * place + core, 0:8, :] = sent
            message_ref[2 * place + core, 8:16, :] = notes


def rows_kernel(inbox_ref, update_ref, kept_ref, rows_ref, ratio_ref):
    notes = inbox_ref[0, 8:16, :]
    for source in range(1, 32):
        notes = notes + inbox_ref[source, 8:16, :]
    lane = lax.broadcasted_iota(jnp.int32, (8, 128), 1)
    weight_sq = jnp.sum(jnp.where(lane == 0, notes, 0.0), keepdims=True)
    update_sq = jnp.sum(jnp.where(lane == 1, notes, 0.0), keepdims=True)
    ratio = jnp.sqrt(weight_sq) / (jnp.sqrt(update_sq) + norm_eps)
    ratio_ref[...] = jnp.broadcast_to(ratio, (8, 128))
    for start in range(0, update_ref.shape[1], CHUNK):
        part = pl.ds(start, CHUNK)
        rows = (kept_ref[:, part] - rate * ratio * update_ref[:, part]).astype(jnp.bfloat16)
        for place in range(16):
            rows_ref[place, :, part] = rows


def place_kernel(at_ref, rows_ref, *refs):
    out_ref, held, in_sems, out_sems = refs[-4:]
    reads = [pltpu.make_async_copy(rows_ref.at[i], held.at[i], in_sems.at[i]) for i in range(16)]
    writes = [
        pltpu.make_async_copy(held.at[i], out_ref.at[i, at_ref[0]], out_sems.at[i])
        for i in range(16)
    ]
    for read in reads:
        read.start()
    for read, write in zip(reads, writes):
        read.wait()
        write.start()
    for write in writes:
        write.wait()


def place(at, rows, *partly):
    shape = (16, 2) + rows.shape[1:]
    return pl.pallas_call(
        place_kernel,
        out_shape=jax.ShapeDtypeStruct(shape, rows.dtype),
        in_specs=[SMEM] + [pl.BlockSpec(memory_space=pl.ANY)] * (1 + len(partly)),
        out_specs=pl.BlockSpec(memory_space=pl.ANY),
        scratch_shapes=[
            pltpu.VMEM(rows.shape, rows.dtype),
            pltpu.SemaphoreType.DMA((16,)),
            pltpu.SemaphoreType.DMA((16,)),
        ],
        input_output_aliases={2: 0} if partly else {},
        cost_estimate=pl.CostEstimate(flops=0, bytes_accessed=2 * rows.nbytes, transcendentals=0),
        compiler_params=LIMIT,
        name="place",
    )(at, rows, *partly)


def on_device(grads, basis, weights, moment, second):
    grad = grads[0, 0, 0]
    width = grad.shape[1]
    core = lax.axis_index("c")
    deep = lax.axis_index("z")
    low = lax.axis_index("yl")
    outer = lax.axis_index("yh") * 4 + lax.axis_index("x")
    core_at = core.astype(jnp.int32).reshape(1)

    turned = basis.T
    half = turned.shape[1] // 2
    mine = lax.dynamic_slice_in_dim(turned, half * core, half, 1)
    theirs = swap(lax.dynamic_slice_in_dim(turned, half * (1 - core), half, 1))
    state = pl.pallas_call(
        pack_kernel,
        out_shape=jax.ShapeDtypeStruct((12, width), jnp.bfloat16),
        in_specs=[VMEM, VMEM, VMEM],
        out_specs=VMEM,
        name="pack",
    )(moment, second, weights)
    state_z = lax.all_gather(state, "z")
    chip = in_order(core, mine, theirs, 0).reshape(-1, half)
    part = chip.shape[0] // 8
    piece = lax.dynamic_slice_in_dim(chip, part * outer, part, 0)
    along_z = share(piece, "z", 16)
    other_grad = swap(grad)
    blocks = share(along_z, PLANE, 16)
    blocks = blocks.reshape(2, 8, 16, part, half)
    own_basis = blocks.transpose(0, 2, 1, 3, 4).reshape(width, half)

    sketch = pl.pallas_call(
        product_kernel,
        out_shape=jax.ShapeDtypeStruct((grad.shape[0], half), jnp.float32),
        in_specs=[VMEM, VMEM, VMEM],
        out_specs=VMEM,
        compiler_params=LIMIT,
        name="product",
    )(grad, other_grad, own_basis)
    sketch, basis_sent = lax.optimization_barrier((sketch, own_basis))
    other_basis = swap(basis_sent)
    plane_terms = exchange(sketch.reshape(16, 16, half), PLANE)
    plane_terms, state_z = lax.optimization_barrier((plane_terms, state_z))
    plane_sum = jnp.sum(plane_terms, axis=0)
    spread = jnp.broadcast_to(plane_sum.reshape(2, 1, 8, half), (2, 16, 8, half))
    terms = exchange(spread.reshape(32, 8, half), ("c", "z"))

    state_one = lax.dynamic_index_in_dim(state_z, 2 * outer + core, 0, keepdims=False)
    state_two = swap(lax.dynamic_index_in_dim(state_z, 2 * outer + 1 - core, 0, keepdims=False))
    wide = jax.ShapeDtypeStruct((8, width), jnp.float32)
    update8, kept8, message = pl.pallas_call(
        update_kernel,
        out_shape=(wide, wide, jax.ShapeDtypeStruct((32, 16, half), jnp.float32)),
        in_specs=[SMEM, VMEM, VMEM, VMEM, VMEM, VMEM],
        out_specs=(VMEM, VMEM, VMEM),
        compiler_params=LIMIT,
        name="update",
    )(
        jnp.stack([core, core]).astype(jnp.int32),
        terms,
        own_basis,
        other_basis,
        state_one,
        state_two,
    )
    inbox = exchange(message, PLANE + ("c",))
    rows_out, ratio = pl.pallas_call(
        rows_kernel,
        out_shape=(
            jax.ShapeDtypeStruct((16, 8, width), jnp.bfloat16),
            jax.ShapeDtypeStruct((8, 128), jnp.float32),
        ),
        in_specs=[VMEM, VMEM, VMEM],
        out_specs=(VMEM, VMEM),
        compiler_params=LIMIT,
        name="rows",
    )(inbox, update8, kept8)
    rows_mine = exchange(rows_out, PLANE)
    rows_other = swap(rows_mine)
    partly = place(core_at, rows_mine)
    gathered = place(1 - core_at, rows_other, partly)
    gathered = gathered.reshape(1, 256, width)

    trust_ratio = ratio[0, 0]
    own = lax.dynamic_index_in_dim(inbox, low * 16 + deep, 0, keepdims=False)[:8]
    estimate = estimate_rows(own.reshape(2, 4, half), core, own_basis, other_basis, 3)[None]
    moment_new, second_new, update = moments(estimate, weights, moment, second)
    weight_new = weights - rate * trust_ratio * update
    return (weight_new, moment_new, second_new, gathered)


def solution(mesh):
    fine = Mesh(mesh.devices.reshape(tuple(FINE.values())), tuple(FINE))
    rows = P(None, DP, None)
    return jax.shard_map(
        on_device,
        mesh=fine,
        in_specs=(P(OUTER, DP, None, None, None), P(None, DP), rows, rows, rows),
        out_specs=(rows, rows, rows, P()),
        check_vma=False,
    )
```

```python
import jax
import jax.numpy as jnp
from jax import lax
from jax.experimental import pallas as pl
from jax.experimental.pallas import tpu as pltpu
from jax.sharding import Mesh
from jax.sharding import PartitionSpec as P

beta_one = 0.9
beta_two = 0.999
bias_one = 1.0 - 0.9**10
bias_two = 1.0 - 0.999**10
adam_eps = 1e-06
norm_eps = 1e-06
decay = 0.01
rate = 0.1

FINE = {"yh": 2, "x": 4, "yl": 2, "z": 16, "c": 2}
OUTER = ("yh", "x")
DP = ("yl", "z", "c")
PLANE = ("yl", "yh", "x")
SWAP = [(0, 1), (1, 0)]
ALL = tuple(FINE)


def moves(target):
    pairs = []
    for o in range(8):
        for low in range(2):
            for z in range(16):
                for c in range(2):
                    to_o, to_z, to_c = target(o, z, c)
                    pairs.append(
                        (((o * 2 + low) * 16 + z) * 2 + c, ((to_o * 2 + low) * 16 + to_z) * 2 + to_c)
                    )
    return pairs


def along_z_moves(offset):
    return moves(lambda o, z, c: (o, (o + offset - z) % 16, c))


def in_plane_moves(first):
    def target(o, z, c):
        row = (o + 8 * ((c + first) % 2) - z) % 16
        return row // 2, z, row % 2

    return moves(target)


def exchange(blocks, axes):
    return lax.all_to_all(blocks, axes, 0, 0, tiled=True)


def share(block, axes, count):
    return exchange(jnp.broadcast_to(block[None], (count,) + block.shape), axes)


def swap(block):
    return lax.ppermute(block, "c", SWAP)


def in_order(position, mine, other, axis):
    shape = [1] * (mine.ndim + 1)
    shape[axis] = 2
    here = (jnp.arange(2) == position).reshape(shape)
    return jnp.where(here, jnp.expand_dims(mine, axis), jnp.expand_dims(other, axis))


def pieces(values, count):
    parts = []
    rest = values
    for _ in range(count):
        part = lax.reduce_precision(rest, 8, 7)
        parts.append(part.astype(jnp.bfloat16))
        rest = rest - part
    return jnp.concatenate(parts, axis=0)


def estimate_rows(halves, core, own_basis, other_basis, count):
    rows = halves.shape[1]
    total = 0.0
    for half, basis in ((core, own_basis), (1 - core, other_basis)):
        left = pieces(lax.dynamic_index_in_dim(halves, half, 0, keepdims=False), count)
        total = total + lax.dot_general(
            left, basis, (((1,), (1,)), ((), ())), preferred_element_type=jnp.float32
        )
    total = total.reshape(count, rows, -1)
    return jnp.sum(total, axis=0) / 256


def moments(estimate, weights, moment, second):
    moment_new = beta_one * moment + (1.0 - beta_one) * estimate
    second_new = beta_two * second + (1.0 - beta_two) * estimate * estimate
    update = moment_new / bias_one / (jnp.sqrt(second_new / bias_two) + adam_eps) + decay * weights
    return moment_new, second_new, update


VMEM = pl.BlockSpec(memory_space=pltpu.VMEM)
SMEM = pl.BlockSpec(memory_space=pltpu.SMEM)
LIMIT = pltpu.CompilerParams(vmem_limit_bytes=6 << 20)
CHUNK = 512


def pack_kernel(moment_ref, second_ref, weights_ref, out_ref):
    rows = [moment_ref[0], second_ref[0], weights_ref[0]]
    out_ref[...] = jnp.concatenate(rows, axis=0).astype(jnp.bfloat16)


def product_kernel(grad_ref, other_ref, basis_ref, out_ref):
    basis = basis_ref[...]
    total = jnp.dot(grad_ref[...], basis, preferred_element_type=jnp.float32)
    out_ref[...] = total + jnp.dot(other_ref[...], basis, preferred_element_type=jnp.float32)


def update_kernel(
    at_ref, terms_ref, own_ref, other_ref, one_ref, two_ref, update_ref, kept_ref, message_ref
):
    first, second = terms_ref[0], terms_ref[16]
    for step in range(1, 16):
        first = first + terms_ref[step]
        second = second + terms_ref[16 + step]
    at_first = at_ref[0] == 0
    one_first = at_ref[1] == 0

    def left_of(half):
        high = half.astype(jnp.bfloat16).astype(jnp.float32)
        return jnp.concatenate([high, half - high], axis=0).astype(jnp.bfloat16)

    left_own = left_of(jnp.where(at_first, first, second))
    left_other = left_of(jnp.where(at_first, second, first))
    contract = (((1,), (1,)), ((), ()))
    weight_sq = jnp.zeros((8, CHUNK), jnp.float32)
    update_sq = jnp.zeros((8, CHUNK), jnp.float32)
    for start in range(0, own_ref.shape[0], CHUNK):
        part = pl.ds(start, CHUNK)
        both = lax.dot_general(
            left_own, own_ref[part, :], contract, preferred_element_type=jnp.float32
        ) + lax.dot_general(
            left_other, other_ref[part, :], contract, preferred_element_type=jnp.float32
        )
        one = one_ref[:, part].astype(jnp.float32)
        two = two_ref[:, part].astype(jnp.float32)
        upper = jnp.where(one_first, one, two)
        lower = jnp.where(one_first, two, one)
        moment, before, weights = [
            jnp.concatenate([upper[r : r + 4], lower[r : r + 4]], axis=0) for r in (0, 4, 8)
        ]
        _, _, update = moments((both[:8] + both[8:]) / 256, weights, moment, before)
        update_ref[:, part] = update
        kept_ref[:, part] = weights
        weight_sq = weight_sq + weights * weights
        update_sq = update_sq + update * update
    row = lax.broadcasted_iota(jnp.int32, (8, 128), 0)
    lane = lax.broadcasted_iota(jnp.int32, (8, 128), 1)
    notes = jnp.where(
        (row == 0) & (lane == 0),
        jnp.sum(weight_sq),
        jnp.where((row == 0) & (lane == 1), jnp.sum(update_sq), 0.0),
    )
    for core in range(2):
        rows = slice(4 * core, 4 * core + 4)
        sent = jnp.concatenate([first[rows], second[rows]], axis=0)
        for place in range(16):
            message_ref[2 * place + core, 0:8, :] = sent
            message_ref[2 * place + core, 8:16, :] = notes


def rows_kernel(inbox_ref, update_ref, kept_ref, rows_ref, ratio_ref):
    notes = inbox_ref[0, 8:16, :]
    for source in range(1, 32):
        notes = notes + inbox_ref[source, 8:16, :]
    lane = lax.broadcasted_iota(jnp.int32, (8, 128), 1)
    weight_sq = jnp.sum(jnp.where(lane == 0, notes, 0.0), keepdims=True)
    update_sq = jnp.sum(jnp.where(lane == 1, notes, 0.0), keepdims=True)
    ratio = jnp.sqrt(weight_sq) / (jnp.sqrt(update_sq) + norm_eps)
    ratio_ref[...] = jnp.broadcast_to(ratio, (8, 128))
    for start in range(0, update_ref.shape[1], CHUNK):
        part = pl.ds(start, CHUNK)
        rows = (kept_ref[:, part] - rate * ratio * update_ref[:, part]).astype(jnp.bfloat16)
        for place in range(16):
            rows_ref[place, :, part] = rows


def place_kernel(at_ref, rows_ref, *refs):
    out_ref, sems = refs[-2:]
    copies = [
        pltpu.make_async_copy(rows_ref.at[i], out_ref.at[i, at_ref[0]], sems.at[i])
        for i in range(16)
    ]
    for copy in copies:
        copy.start()
    for copy in copies:
        copy.wait()


def place(at, rows, *partly):
    shape = (16, 2) + rows.shape[1:]
    return pl.pallas_call(
        place_kernel,
        out_shape=jax.ShapeDtypeStruct(shape, rows.dtype),
        in_specs=[SMEM, VMEM] + [pl.BlockSpec(memory_space=pl.ANY)] * len(partly),
        out_specs=pl.BlockSpec(memory_space=pl.ANY),
        scratch_shapes=[pltpu.SemaphoreType.DMA((16,))],
        input_output_aliases={2: 0} if partly else {},
        cost_estimate=pl.CostEstimate(flops=0, bytes_accessed=2 * rows.nbytes, transcendentals=0),
        compiler_params=LIMIT,
        name="place",
    )(at, rows, *partly)


def on_device(grads, basis, weights, moment, second):
    grad = grads[0, 0, 0]
    width = grad.shape[1]
    core = lax.axis_index("c")
    deep = lax.axis_index("z")
    low = lax.axis_index("yl")
    outer = lax.axis_index("yh") * 4 + lax.axis_index("x")

    turned = basis.T
    half = turned.shape[1] // 2
    mine = lax.dynamic_slice_in_dim(turned, half * core, half, 1)
    theirs = swap(lax.dynamic_slice_in_dim(turned, half * (1 - core), half, 1))
    chip = in_order(core, mine, theirs, 0).reshape(-1, half)
    part = chip.shape[0] // 8
    piece = lax.dynamic_slice_in_dim(chip, part * outer, part, 0)
    along_z = share(piece, "z", 16)
    along_z, m_in, v_in, w_in = lax.optimization_barrier((along_z, moment, second, weights))
    state = pl.pallas_call(
        pack_kernel,
        out_shape=jax.ShapeDtypeStruct((12, width), jnp.bfloat16),
        in_specs=[VMEM, VMEM, VMEM],
        out_specs=VMEM,
        name="pack",
    )(m_in, v_in, w_in)
    state_a = lax.ppermute(state, ALL, along_z_moves(0))
    state_b = lax.ppermute(state, ALL, along_z_moves(8))
    other_grad = swap(grad)
    blocks = share(along_z, PLANE, 16)
    blocks, state_a, state_b = lax.optimization_barrier((blocks, state_a, state_b))
    blocks = blocks.reshape(2, 8, 16, part, half)
    own_basis = blocks.transpose(0, 2, 1, 3, 4).reshape(width, half)

    sketch = pl.pallas_call(
        product_kernel,
        out_shape=jax.ShapeDtypeStruct((grad.shape[0], half), jnp.float32),
        in_specs=[VMEM, VMEM, VMEM],
        out_specs=VMEM,
        compiler_params=LIMIT,
        name="product",
    )(grad, other_grad, own_basis)
    sketch, basis_sent = lax.optimization_barrier((sketch, own_basis))
    other_basis = swap(basis_sent)
    plane_terms = exchange(sketch.reshape(16, 16, half), PLANE)
    plane_sum = jnp.sum(plane_terms, axis=0)
    plane_sum, state_a, state_b = lax.optimization_barrier((plane_sum, state_a, state_b))
    state_one = lax.ppermute(jnp.where(core == 0, state_a, state_b), ALL, in_plane_moves(0))
    state_two = lax.ppermute(jnp.where(core == 0, state_b, state_a), ALL, in_plane_moves(1))
    spread = jnp.broadcast_to(plane_sum.reshape(2, 1, 8, half), (2, 16, 8, half))
    terms = exchange(spread.reshape(32, 8, half), ("c", "z"))

    wide = jax.ShapeDtypeStruct((8, width), jnp.float32)
    update8, kept8, message = pl.pallas_call(
        update_kernel,
        out_shape=(wide, wide, jax.ShapeDtypeStruct((32, 16, half), jnp.float32)),
        in_specs=[SMEM, VMEM, VMEM, VMEM, VMEM, VMEM],
        out_specs=(VMEM, VMEM, VMEM),
        compiler_params=LIMIT,
        name="update",
    )(
        jnp.stack([core, (2 * outer + core + deep) % 16 // 8]).astype(jnp.int32),
        terms,
        own_basis,
        other_basis,
        state_one,
        state_two,
    )
    inbox = exchange(message, PLANE + ("c",))
    rows_out, ratio = pl.pallas_call(
        rows_kernel,
        out_shape=(
            jax.ShapeDtypeStruct((16, 8, width), jnp.bfloat16),
            jax.ShapeDtypeStruct((8, 128), jnp.float32),
        ),
        in_specs=[VMEM, VMEM, VMEM],
        out_specs=(VMEM, VMEM),
        compiler_params=LIMIT,
        name="rows",
    )(inbox, update8, kept8)
    rows_mine = exchange(rows_out, PLANE)

    trust_ratio = ratio[0, 0]
    own = lax.dynamic_index_in_dim(inbox, low * 16 + deep, 0, keepdims=False)[:8]
    estimate = estimate_rows(own.reshape(2, 4, half), core, own_basis, other_basis, 3)[None]
    moment_new, second_new, update = moments(estimate, weights, moment, second)
    weight_new = weights - rate * trust_ratio * update
    rows_mine, weight_new, moment_new, second_new = lax.optimization_barrier(
        (rows_mine, weight_new, moment_new, second_new)
    )
    rows_other = swap(rows_mine)
    core_at = core.astype(jnp.int32).reshape(1)
    gathered = place(1 - core_at, rows_other, place(core_at, rows_mine)).reshape(1, 256, width)
    return (weight_new, moment_new, second_new, gathered)


def solution(mesh):
    fine = Mesh(mesh.devices.reshape(tuple(FINE.values())), tuple(FINE))
    rows = P(None, DP, None)
    return jax.shard_map(
        on_device,
        mesh=fine,
        in_specs=(P(OUTER, DP, None, None, None), P(None, DP), rows, rows, rows),
        out_specs=(rows, rows, rows, P()),
        check_vma=False,
    )
```

```python
import jax
import jax.numpy as jnp
from jax import lax
from jax.experimental import pallas as pl
from jax.experimental.pallas import tpu as pltpu
from jax.sharding import Mesh
from jax.sharding import PartitionSpec as P

beta_one = 0.9
beta_two = 0.999
bias_one = 1.0 - 0.9**10
bias_two = 1.0 - 0.999**10
adam_eps = 1e-06
norm_eps = 1e-06
decay = 0.01
rate = 0.1

FINE = {"yh": 2, "x": 4, "yl": 2, "z": 16, "c": 2}
OUTER = ("yh", "x")
DP = ("yl", "z", "c")
PLANE = ("yl", "yh", "x")
SWAP = [(0, 1), (1, 0)]
ALL = tuple(FINE)


def moves(target):
    pairs = []
    for o in range(8):
        for low in range(2):
            for z in range(16):
                for c in range(2):
                    to_o, to_z, to_c = target(o, z, c)
                    pairs.append(
                        (((o * 2 + low) * 16 + z) * 2 + c, ((to_o * 2 + low) * 16 + to_z) * 2 + to_c)
                    )
    return pairs


def along_z_moves(first):
    return moves(lambda o, z, c: (o, (o + 8 * ((c + first) % 2) - z) % 16, c))


def in_plane_moves(first):
    def target(o, z, c):
        row = (o + 8 * ((c + first) % 2) - z) % 16
        return row // 2, z, row % 2

    return moves(target)


def exchange(blocks, axes):
    return lax.all_to_all(blocks, axes, 0, 0, tiled=True)


def share(block, axes, count):
    return exchange(jnp.broadcast_to(block[None], (count,) + block.shape), axes)


def swap(block):
    return lax.ppermute(block, "c", SWAP)


def in_order(position, mine, other, axis):
    shape = [1] * (mine.ndim + 1)
    shape[axis] = 2
    here = (jnp.arange(2) == position).reshape(shape)
    return jnp.where(here, jnp.expand_dims(mine, axis), jnp.expand_dims(other, axis))


def pieces(values, count):
    parts = []
    rest = values
    for _ in range(count):
        part = lax.reduce_precision(rest, 8, 7)
        parts.append(part.astype(jnp.bfloat16))
        rest = rest - part
    return jnp.concatenate(parts, axis=0)


def estimate_rows(halves, core, own_basis, other_basis, count):
    rows = halves.shape[1]
    total = 0.0
    for half, basis in ((core, own_basis), (1 - core, other_basis)):
        left = pieces(lax.dynamic_index_in_dim(halves, half, 0, keepdims=False), count)
        total = total + lax.dot_general(
            left, basis, (((1,), (1,)), ((), ())), preferred_element_type=jnp.float32
        )
    total = total.reshape(count, rows, -1)
    return jnp.sum(total, axis=0) / 256


def moments(estimate, weights, moment, second):
    moment_new = beta_one * moment + (1.0 - beta_one) * estimate
    second_new = beta_two * second + (1.0 - beta_two) * estimate * estimate
    update = moment_new / bias_one / (jnp.sqrt(second_new / bias_two) + adam_eps) + decay * weights
    return moment_new, second_new, update


VMEM = pl.BlockSpec(memory_space=pltpu.VMEM)
SMEM = pl.BlockSpec(memory_space=pltpu.SMEM)
LIMIT = pltpu.CompilerParams(vmem_limit_bytes=6 << 20)
CHUNK = 512


def pack_kernel(moment_ref, second_ref, weights_ref, out_ref):
    rows = [moment_ref[0], second_ref[0], weights_ref[0]]
    out_ref[...] = jnp.concatenate(rows, axis=0).astype(jnp.bfloat16)


def product_kernel(grad_ref, other_ref, basis_ref, out_ref):
    basis = basis_ref[...]
    total = jnp.dot(grad_ref[...], basis, preferred_element_type=jnp.float32)
    out_ref[...] = total + jnp.dot(other_ref[...], basis, preferred_element_type=jnp.float32)


def update_kernel(
    at_ref, terms_ref, own_ref, other_ref, one_ref, two_ref, update_ref, kept_ref, message_ref
):
    first, second = terms_ref[0], terms_ref[16]
    for step in range(1, 16):
        first = first + terms_ref[step]
        second = second + terms_ref[16 + step]
    at_first = at_ref[0] == 0
    one_first = at_ref[1] == 0

    def left_of(half):
        high = half.astype(jnp.bfloat16).astype(jnp.float32)
        return jnp.concatenate([high, half - high], axis=0).astype(jnp.bfloat16)

    left_own = left_of(jnp.where(at_first, first, second))
    left_other = left_of(jnp.where(at_first, second, first))
    contract = (((1,), (1,)), ((), ()))
    weight_sq = jnp.zeros((8, CHUNK), jnp.float32)
    update_sq = jnp.zeros((8, CHUNK), jnp.float32)
    for start in range(0, own_ref.shape[0], CHUNK):
        part = pl.ds(start, CHUNK)
        both = lax.dot_general(
            left_own, own_ref[part, :], contract, preferred_element_type=jnp.float32
        ) + lax.dot_general(
            left_other, other_ref[part, :], contract, preferred_element_type=jnp.float32
        )
        one = one_ref[:, part].astype(jnp.float32)
        two = two_ref[:, part].astype(jnp.float32)
        upper = jnp.where(one_first, one, two)
        lower = jnp.where(one_first, two, one)
        moment, before, weights = [
            jnp.concatenate([upper[r : r + 4], lower[r : r + 4]], axis=0) for r in (0, 4, 8)
        ]
        _, _, update = moments((both[:8] + both[8:]) / 256, weights, moment, before)
        update_ref[:, part] = update
        kept_ref[:, part] = weights
        weight_sq = weight_sq + weights * weights
        update_sq = update_sq + update * update
    row = lax.broadcasted_iota(jnp.int32, (8, 128), 0)
    lane = lax.broadcasted_iota(jnp.int32, (8, 128), 1)
    notes = jnp.where(
        (row == 0) & (lane == 0),
        jnp.sum(weight_sq),
        jnp.where((row == 0) & (lane == 1), jnp.sum(update_sq), 0.0),
    )
    for core in range(2):
        rows = slice(4 * core, 4 * core + 4)
        sent = jnp.concatenate([first[rows], second[rows]], axis=0)
        for place in range(16):
            message_ref[2 * place + core, 0:8, :] = sent
            message_ref[2 * place + core, 8:16, :] = notes


def rows_kernel(inbox_ref, update_ref, kept_ref, rows_ref, ratio_ref):
    notes = inbox_ref[0, 8:16, :]
    for source in range(1, 32):
        notes = notes + inbox_ref[source, 8:16, :]
    lane = lax.broadcasted_iota(jnp.int32, (8, 128), 1)
    weight_sq = jnp.sum(jnp.where(lane == 0, notes, 0.0), keepdims=True)
    update_sq = jnp.sum(jnp.where(lane == 1, notes, 0.0), keepdims=True)
    ratio = jnp.sqrt(weight_sq) / (jnp.sqrt(update_sq) + norm_eps)
    ratio_ref[...] = jnp.broadcast_to(ratio, (8, 128))
    for start in range(0, update_ref.shape[1], CHUNK):
        part = pl.ds(start, CHUNK)
        rows = (kept_ref[:, part] - rate * ratio * update_ref[:, part]).astype(jnp.bfloat16)
        for place in range(16):
            rows_ref[place, :, part] = rows


def place_kernel(at_ref, rows_ref, *refs):
    out_ref, sems = refs[-2:]
    copies = [
        pltpu.make_async_copy(rows_ref.at[i], out_ref.at[i, at_ref[0]], sems.at[i])
        for i in range(16)
    ]
    for copy in copies:
        copy.start()
    for copy in copies:
        copy.wait()


def place(at, rows, *partly):
    shape = (16, 2) + rows.shape[1:]
    return pl.pallas_call(
        place_kernel,
        out_shape=jax.ShapeDtypeStruct(shape, rows.dtype),
        in_specs=[SMEM, VMEM] + [pl.BlockSpec(memory_space=pl.ANY)] * len(partly),
        out_specs=pl.BlockSpec(memory_space=pl.ANY),
        scratch_shapes=[pltpu.SemaphoreType.DMA((16,))],
        input_output_aliases={2: 0} if partly else {},
        cost_estimate=pl.CostEstimate(flops=0, bytes_accessed=2 * rows.nbytes, transcendentals=0),
        compiler_params=LIMIT,
        name="place",
    )(at, rows, *partly)


def on_device(grads, basis, weights, moment, second):
    grad = grads[0, 0, 0]
    width = grad.shape[1]
    core = lax.axis_index("c")
    deep = lax.axis_index("z")
    low = lax.axis_index("yl")
    outer = lax.axis_index("yh") * 4 + lax.axis_index("x")

    turned = basis.T
    half = turned.shape[1] // 2
    mine = lax.dynamic_slice_in_dim(turned, half * core, half, 1)
    theirs = swap(lax.dynamic_slice_in_dim(turned, half * (1 - core), half, 1))
    chip = in_order(core, mine, theirs, 0).reshape(-1, half)
    part = chip.shape[0] // 8
    piece = lax.dynamic_slice_in_dim(chip, part * outer, part, 0)
    along_z = share(piece, "z", 16)
    along_z, m_in, v_in, w_in = lax.optimization_barrier((along_z, moment, second, weights))
    state = pl.pallas_call(
        pack_kernel,
        out_shape=jax.ShapeDtypeStruct((12, width), jnp.bfloat16),
        in_specs=[VMEM, VMEM, VMEM],
        out_specs=VMEM,
        name="pack",
    )(m_in, v_in, w_in)
    came_one = lax.ppermute(state, ALL, along_z_moves(0))
    other_grad = swap(grad)
    blocks = share(along_z, PLANE, 16)
    blocks, came_one = lax.optimization_barrier((blocks, came_one))
    blocks = blocks.reshape(2, 8, 16, part, half)
    own_basis = blocks.transpose(0, 2, 1, 3, 4).reshape(width, half)

    sketch = pl.pallas_call(
        product_kernel,
        out_shape=jax.ShapeDtypeStruct((grad.shape[0], half), jnp.float32),
        in_specs=[VMEM, VMEM, VMEM],
        out_specs=VMEM,
        compiler_params=LIMIT,
        name="product",
    )(grad, other_grad, own_basis)
    sketch, basis_sent, state, came_one = lax.optimization_barrier(
        (sketch, own_basis, state, came_one)
    )
    came_two = lax.ppermute(state, ALL, along_z_moves(1))
    state_one = lax.ppermute(came_one, ALL, in_plane_moves(0))
    other_basis = swap(basis_sent)
    plane_terms = exchange(sketch.reshape(16, 16, half), PLANE)
    plane_terms, came_two = lax.optimization_barrier((plane_terms, came_two))
    plane_sum = jnp.sum(plane_terms, axis=0)
    state_two = lax.ppermute(came_two, ALL, in_plane_moves(1))
    spread = jnp.broadcast_to(plane_sum.reshape(2, 1, 8, half), (2, 16, 8, half))
    terms = exchange(spread.reshape(32, 8, half), ("c", "z"))

    wide = jax.ShapeDtypeStruct((8, width), jnp.float32)
    update8, kept8, message = pl.pallas_call(
        update_kernel,
        out_shape=(wide, wide, jax.ShapeDtypeStruct((32, 16, half), jnp.float32)),
        in_specs=[SMEM, VMEM, VMEM, VMEM, VMEM, VMEM],
        out_specs=(VMEM, VMEM, VMEM),
        compiler_params=LIMIT,
        name="update",
    )(
        jnp.stack([core, (2 * outer + core + deep) % 16 // 8]).astype(jnp.int32),
        terms,
        own_basis,
        other_basis,
        state_one,
        state_two,
    )
    inbox = exchange(message, PLANE + ("c",))
    rows_out, ratio = pl.pallas_call(
        rows_kernel,
        out_shape=(
            jax.ShapeDtypeStruct((16, 8, width), jnp.bfloat16),
            jax.ShapeDtypeStruct((8, 128), jnp.float32),
        ),
        in_specs=[VMEM, VMEM, VMEM],
        out_specs=(VMEM, VMEM),
        compiler_params=LIMIT,
        name="rows",
    )(inbox, update8, kept8)
    rows_mine = exchange(rows_out, PLANE)

    trust_ratio = ratio[0, 0]
    own = lax.dynamic_index_in_dim(inbox, low * 16 + deep, 0, keepdims=False)[:8]
    estimate = estimate_rows(own.reshape(2, 4, half), core, own_basis, other_basis, 3)[None]
    moment_new, second_new, update = moments(estimate, weights, moment, second)
    weight_new = weights - rate * trust_ratio * update
    rows_mine, weight_new, moment_new, second_new = lax.optimization_barrier(
        (rows_mine, weight_new, moment_new, second_new)
    )
    rows_other = swap(rows_mine)
    core_at = core.astype(jnp.int32).reshape(1)
    gathered = place(1 - core_at, rows_other, place(core_at, rows_mine)).reshape(1, 256, width)
    return (weight_new, moment_new, second_new, gathered)


def solution(mesh):
    fine = Mesh(mesh.devices.reshape(tuple(FINE.values())), tuple(FINE))
    rows = P(None, DP, None)
    return jax.shard_map(
        on_device,
        mesh=fine,
        in_specs=(P(OUTER, DP, None, None, None), P(None, DP), rows, rows, rows),
        out_specs=(rows, rows, rows, P()),
        check_vma=False,
    )
```

```python
import functools

import jax
import jax.numpy as jnp
from jax import lax
from jax.experimental import pallas as pl
from jax.experimental.pallas import tpu as pltpu
from jax.sharding import Mesh
from jax.sharding import PartitionSpec as P

beta_one = 0.9
beta_two = 0.999
bias_one = 1.0 - 0.9**10
bias_two = 1.0 - 0.999**10
adam_eps = 1e-06
norm_eps = 1e-06
decay = 0.01
rate = 0.1

FINE = {"yh": 2, "x": 4, "yl": 2, "z": 16, "c": 2}
OUTER = ("yh", "x")
DP = ("yl", "z", "c")
PLANE = ("yl", "yh", "x")
SWAP = [(0, 1), (1, 0)]
ALL = tuple(FINE)


def moves(target):
    pairs = []
    for o in range(8):
        for low in range(2):
            for z in range(16):
                for c in range(2):
                    to_o, to_z, to_c = target(o, z, c)
                    pairs.append(
                        (((o * 2 + low) * 16 + z) * 2 + c, ((to_o * 2 + low) * 16 + to_z) * 2 + to_c)
                    )
    return pairs


def along_z_moves(first):
    return moves(lambda o, z, c: (o, (o + 8 * ((c + first) % 2) - z) % 16, c))


def in_plane_moves(first):
    def target(o, z, c):
        row = (o + 8 * ((c + first) % 2) - z) % 16
        return row // 2, z, row % 2

    return moves(target)


def exchange(blocks, axes):
    return lax.all_to_all(blocks, axes, 0, 0, tiled=True)


def share(block, axes, count):
    return exchange(jnp.broadcast_to(block[None], (count,) + block.shape), axes)


def swap(block):
    return lax.ppermute(block, "c", SWAP)


def in_order(position, mine, other, axis):
    shape = [1] * (mine.ndim + 1)
    shape[axis] = 2
    here = (jnp.arange(2) == position).reshape(shape)
    return jnp.where(here, jnp.expand_dims(mine, axis), jnp.expand_dims(other, axis))


def moments(estimate, weights, moment, second):
    moment_new = beta_one * moment + (1.0 - beta_one) * estimate
    second_new = beta_two * second + (1.0 - beta_two) * estimate * estimate
    update = moment_new / bias_one / (jnp.sqrt(second_new / bias_two) + adam_eps) + decay * weights
    return moment_new, second_new, update


VMEM = pl.BlockSpec(memory_space=pltpu.VMEM)
SMEM = pl.BlockSpec(memory_space=pltpu.SMEM)
LIMIT = pltpu.CompilerParams(vmem_limit_bytes=6 << 20)
CHUNK = 512


def pack_kernel(moment_ref, second_ref, weights_ref, out_ref):
    rows = [moment_ref[0], second_ref[0], weights_ref[0]]
    out_ref[...] = jnp.concatenate(rows, axis=0).astype(jnp.bfloat16)


def product_kernel(grad_ref, other_ref, basis_ref, out_ref):
    basis = basis_ref[...]
    total = jnp.dot(grad_ref[...], basis, preferred_element_type=jnp.float32)
    out_ref[...] = total + jnp.dot(other_ref[...], basis, preferred_element_type=jnp.float32)


def update_kernel(
    at_ref, terms_ref, own_ref, other_ref, one_ref, two_ref, update_ref, kept_ref, message_ref
):
    first, second = terms_ref[0], terms_ref[16]
    for step in range(1, 16):
        first = first + terms_ref[step]
        second = second + terms_ref[16 + step]
    at_first = at_ref[0] == 0
    one_first = at_ref[1] == 0

    def left_of(half):
        high = half.astype(jnp.bfloat16).astype(jnp.float32)
        return jnp.concatenate([high, half - high], axis=0).astype(jnp.bfloat16)

    left_own = left_of(jnp.where(at_first, first, second))
    left_other = left_of(jnp.where(at_first, second, first))
    contract = (((1,), (1,)), ((), ()))
    weight_sq = jnp.zeros((8, CHUNK), jnp.float32)
    update_sq = jnp.zeros((8, CHUNK), jnp.float32)
    for start in range(0, own_ref.shape[0], CHUNK):
        part = pl.ds(start, CHUNK)
        both = lax.dot_general(
            left_own, own_ref[part, :], contract, preferred_element_type=jnp.float32
        ) + lax.dot_general(
            left_other, other_ref[part, :], contract, preferred_element_type=jnp.float32
        )
        one = one_ref[:, part].astype(jnp.float32)
        two = two_ref[:, part].astype(jnp.float32)
        upper = jnp.where(one_first, one, two)
        lower = jnp.where(one_first, two, one)
        moment, before, weights = [
            jnp.concatenate([upper[r : r + 4], lower[r : r + 4]], axis=0) for r in (0, 4, 8)
        ]
        _, _, update = moments((both[:8] + both[8:]) / 256, weights, moment, before)
        update_ref[:, part] = update
        kept_ref[:, part] = weights
        weight_sq = weight_sq + weights * weights
        update_sq = update_sq + update * update
    row = lax.broadcasted_iota(jnp.int32, (8, 128), 0)
    lane = lax.broadcasted_iota(jnp.int32, (8, 128), 1)
    notes = jnp.where(
        (row == 0) & (lane == 0),
        jnp.sum(weight_sq),
        jnp.where((row == 0) & (lane == 1), jnp.sum(update_sq), 0.0),
    )
    for core in range(2):
        rows = slice(4 * core, 4 * core + 4)
        sent = jnp.concatenate([first[rows], second[rows]], axis=0)
        for place in range(16):
            message_ref[2 * place + core, 0:8, :] = sent
            message_ref[2 * place + core, 8:16, :] = notes


def rows_kernel(
    at_ref, inbox_ref, update_ref, kept_ref, rows_ref, ratio_ref, own_left_ref, other_left_ref
):
    sketch = inbox_ref[at_ref[2], 0:8, :]
    swapped = jnp.concatenate([sketch[4:8], sketch[0:4]], axis=0)
    mine_first = jnp.where(at_ref[0] == 0, sketch, swapped)
    high = mine_first.astype(jnp.bfloat16).astype(jnp.float32)
    rest = mine_first - high
    middle = rest.astype(jnp.bfloat16).astype(jnp.float32)
    parts = (high, middle, rest - middle)
    for ref, rows in ((own_left_ref, slice(0, 4)), (other_left_ref, slice(4, 8))):
        ref[...] = jnp.concatenate([p[rows] for p in parts], axis=0).astype(jnp.bfloat16)
    notes = inbox_ref[0, 8:16, :]
    for source in range(1, 32):
        notes = notes + inbox_ref[source, 8:16, :]
    lane = lax.broadcasted_iota(jnp.int32, (8, 128), 1)
    weight_sq = jnp.sum(jnp.where(lane == 0, notes, 0.0), keepdims=True)
    update_sq = jnp.sum(jnp.where(lane == 1, notes, 0.0), keepdims=True)
    ratio = jnp.sqrt(weight_sq) / (jnp.sqrt(update_sq) + norm_eps)
    ratio_ref[...] = jnp.broadcast_to(ratio, (8, 128))
    for start in range(0, update_ref.shape[1], CHUNK):
        part = pl.ds(start, CHUNK)
        rows = (kept_ref[:, part] - rate * ratio * update_ref[:, part]).astype(jnp.bfloat16)
        for place in range(16):
            rows_ref[place, :, part] = rows


def place_kernel(which, at_ref, rows_ref, *refs):
    out_ref, sems = refs[-2:]
    copies = [
        pltpu.make_async_copy(rows_ref.at[i], out_ref.at[i, at_ref[which]], sems.at[i])
        for i in range(16)
    ]
    for copy in copies:
        copy.start()
    for copy in copies:
        copy.wait()


def place(which, at, rows, *partly):
    shape = (16, 2) + rows.shape[1:]
    return pl.pallas_call(
        functools.partial(place_kernel, which),
        out_shape=jax.ShapeDtypeStruct(shape, rows.dtype),
        in_specs=[SMEM, VMEM] + [pl.BlockSpec(memory_space=pl.ANY)] * len(partly),
        out_specs=pl.BlockSpec(memory_space=pl.ANY),
        scratch_shapes=[pltpu.SemaphoreType.DMA((16,))],
        input_output_aliases={2: 0} if partly else {},
        cost_estimate=pl.CostEstimate(flops=0, bytes_accessed=2 * rows.nbytes, transcendentals=0),
        compiler_params=LIMIT,
        name="place",
    )(at, rows, *partly)


def on_device(grads, basis, weights, moment, second):
    grad = grads[0, 0, 0]
    width = grad.shape[1]
    core = lax.axis_index("c")
    deep = lax.axis_index("z")
    low = lax.axis_index("yl")
    outer = lax.axis_index("yh") * 4 + lax.axis_index("x")

    turned = basis.T
    half = turned.shape[1] // 2
    mine = lax.dynamic_slice_in_dim(turned, half * core, half, 1)
    theirs = swap(lax.dynamic_slice_in_dim(turned, half * (1 - core), half, 1))
    chip = in_order(core, mine, theirs, 0).reshape(-1, half)
    part = chip.shape[0] // 8
    piece = lax.dynamic_slice_in_dim(chip, part * outer, part, 0)
    at = jnp.stack([core, (2 * outer + core + deep) % 16 // 8, low * 16 + deep, 1 - core])
    piece, at = lax.optimization_barrier((piece, at.astype(jnp.int32)))
    along_z = share(piece, "z", 16)
    along_z, m_in, v_in, w_in = lax.optimization_barrier((along_z, moment, second, weights))
    state = pl.pallas_call(
        pack_kernel,
        out_shape=jax.ShapeDtypeStruct((12, width), jnp.bfloat16),
        in_specs=[VMEM, VMEM, VMEM],
        out_specs=VMEM,
        compiler_params=LIMIT,
        name="pack",
    )(m_in, v_in, w_in)
    came_one = lax.ppermute(state, ALL, along_z_moves(0))
    other_grad = swap(grad)
    blocks = share(along_z, PLANE, 16)
    blocks, came_one = lax.optimization_barrier((blocks, came_one))
    blocks = blocks.reshape(2, 8, 16, part, half)
    own_basis = blocks.transpose(0, 2, 1, 3, 4).reshape(width, half)

    sketch = pl.pallas_call(
        product_kernel,
        out_shape=jax.ShapeDtypeStruct((grad.shape[0], half), jnp.float32),
        in_specs=[VMEM, VMEM, VMEM],
        out_specs=VMEM,
        compiler_params=LIMIT,
        name="product",
    )(grad, other_grad, own_basis)
    sketch, state, came_one = lax.optimization_barrier((sketch, state, came_one))
    came_two = lax.ppermute(state, ALL, along_z_moves(1))
    state_one = lax.ppermute(came_one, ALL, in_plane_moves(0))
    plane_terms = exchange(sketch.reshape(16, 16, half), PLANE)
    plane_terms, came_two, basis_sent = lax.optimization_barrier(
        (plane_terms, came_two, own_basis)
    )
    other_basis = swap(basis_sent)
    plane_sum = jnp.sum(plane_terms, axis=0)
    state_two = lax.ppermute(came_two, ALL, in_plane_moves(1))
    spread = jnp.broadcast_to(plane_sum.reshape(2, 1, 8, half), (2, 16, 8, half))
    terms = exchange(spread.reshape(32, 8, half), ("c", "z"))

    wide = jax.ShapeDtypeStruct((8, width), jnp.float32)
    update8, kept8, message = pl.pallas_call(
        update_kernel,
        out_shape=(wide, wide, jax.ShapeDtypeStruct((32, 16, half), jnp.float32)),
        in_specs=[SMEM, VMEM, VMEM, VMEM, VMEM, VMEM],
        out_specs=(VMEM, VMEM, VMEM),
        compiler_params=LIMIT,
        name="update",
    )(
        at,
        terms,
        own_basis,
        other_basis,
        state_one,
        state_two,
    )
    inbox = exchange(message, PLANE + ("c",))
    left = jax.ShapeDtypeStruct((12, half), jnp.bfloat16)
    rows_out, ratio, own_left, other_left = pl.pallas_call(
        rows_kernel,
        out_shape=(
            jax.ShapeDtypeStruct((16, 8, width), jnp.bfloat16),
            jax.ShapeDtypeStruct((8, 128), jnp.float32),
            left,
            left,
        ),
        in_specs=[SMEM, VMEM, VMEM, VMEM],
        out_specs=(VMEM, VMEM, VMEM, VMEM),
        compiler_params=LIMIT,
        name="rows",
    )(at, inbox, update8, kept8)
    rows_mine = exchange(rows_out, PLANE)
    rows_mine, ratio, own_left, other_left = lax.optimization_barrier(
        (rows_mine, ratio, own_left, other_left)
    )
    rows_other = swap(rows_mine)
    gathered = place(3, at, rows_other, place(0, at, rows_mine)).reshape(1, 256, width)

    trust_ratio = ratio[0, 0]
    turn = (((1,), (1,)), ((), ()))
    estimate = lax.dot_general(own_left, own_basis, turn, preferred_element_type=jnp.float32)
    estimate = estimate + lax.dot_general(
        other_left, other_basis, turn, preferred_element_type=jnp.float32
    )
    estimate = (estimate[0:4] + estimate[4:8] + estimate[8:12])[None] / 256
    moment_new, second_new, update = moments(estimate, weights, moment, second)
    weight_new = weights - rate * trust_ratio * update
    return (weight_new, moment_new, second_new, gathered)


def solution(mesh):
    fine = Mesh(mesh.devices.reshape(tuple(FINE.values())), tuple(FINE))
    rows = P(None, DP, None)
    return jax.shard_map(
        on_device,
        mesh=fine,
        in_specs=(P(OUTER, DP, None, None, None), P(None, DP), rows, rows, rows),
        out_specs=(rows, rows, rows, P()),
        check_vma=False,
    )
```

```python
import functools

import jax
import jax.numpy as jnp
from jax import lax
from jax.experimental import pallas as pl
from jax.experimental.pallas import tpu as pltpu
from jax.sharding import Mesh
from jax.sharding import PartitionSpec as P

beta_one = 0.9
beta_two = 0.999
bias_one = 1.0 - 0.9**10
bias_two = 1.0 - 0.999**10
adam_eps = 1e-06
norm_eps = 1e-06
decay = 0.01
rate = 0.1

FINE = {"yh": 2, "x": 4, "yl": 2, "z": 16, "c": 2}
OUTER = ("yh", "x")
DP = ("yl", "z", "c")
PLANE = ("yl", "yh", "x")
X_FIRST = ("x", "yh", "yl")
SWAP = [(0, 1), (1, 0)]
ALL = tuple(FINE)


def moves(target):
    pairs = []
    for o in range(8):
        for low in range(2):
            for z in range(16):
                for c in range(2):
                    to_o, to_z, to_c = target(o, z, c)
                    pairs.append(
                        (((o * 2 + low) * 16 + z) * 2 + c, ((to_o * 2 + low) * 16 + to_z) * 2 + to_c)
                    )
    return pairs


def along_z_moves(first):
    return moves(lambda o, z, c: (o, (o + 8 * ((c + first) % 2) - z) % 16, c))


def in_plane_moves(first):
    def target(o, z, c):
        row = (o + 8 * ((c + first) % 2) - z) % 16
        return row // 2, z, row % 2

    return moves(target)


def exchange(blocks, axes):
    return lax.all_to_all(blocks, axes, 0, 0, tiled=True)


def share(block, axes, count):
    return exchange(jnp.broadcast_to(block[None], (count,) + block.shape), axes)


def swap(block):
    return lax.ppermute(block, "c", SWAP)


def in_order(position, mine, other, axis):
    shape = [1] * (mine.ndim + 1)
    shape[axis] = 2
    here = (jnp.arange(2) == position).reshape(shape)
    return jnp.where(here, jnp.expand_dims(mine, axis), jnp.expand_dims(other, axis))


def moments(estimate, weights, moment, second):
    moment_new = beta_one * moment + (1.0 - beta_one) * estimate
    second_new = beta_two * second + (1.0 - beta_two) * estimate * estimate
    update = moment_new / bias_one / (jnp.sqrt(second_new / bias_two) + adam_eps) + decay * weights
    return moment_new, second_new, update


VMEM = pl.BlockSpec(memory_space=pltpu.VMEM)
SMEM = pl.BlockSpec(memory_space=pltpu.SMEM)
LIMIT = pltpu.CompilerParams(vmem_limit_bytes=6 << 20)
CHUNK = 512


def pack_kernel(moment_ref, second_ref, weights_ref, out_ref):
    rows = [moment_ref[0], second_ref[0], weights_ref[0]]
    out_ref[...] = jnp.concatenate(rows, axis=0).astype(jnp.bfloat16)


def product_kernel(grad_ref, other_ref, basis_ref, out_ref):
    basis = basis_ref[...]
    total = jnp.dot(grad_ref[...], basis, preferred_element_type=jnp.float32)
    out_ref[...] = total + jnp.dot(other_ref[...], basis, preferred_element_type=jnp.float32)


def update_kernel(
    at_ref, terms_ref, own_ref, other_ref, one_ref, two_ref, update_ref, kept_ref, message_ref
):
    first, second = terms_ref[0], terms_ref[16]
    for step in range(1, 16):
        first = first + terms_ref[step]
        second = second + terms_ref[16 + step]
    at_first = at_ref[0] == 0
    one_first = at_ref[1] == 0

    def left_of(half):
        high = half.astype(jnp.bfloat16).astype(jnp.float32)
        return jnp.concatenate([high, half - high], axis=0).astype(jnp.bfloat16)

    left_own = left_of(jnp.where(at_first, first, second))
    left_other = left_of(jnp.where(at_first, second, first))
    contract = (((1,), (1,)), ((), ()))
    weight_sq = jnp.zeros((8, CHUNK), jnp.float32)
    update_sq = jnp.zeros((8, CHUNK), jnp.float32)
    for start in range(0, own_ref.shape[0], CHUNK):
        part = pl.ds(start, CHUNK)
        both = lax.dot_general(
            left_own, own_ref[part, :], contract, preferred_element_type=jnp.float32
        ) + lax.dot_general(
            left_other, other_ref[part, :], contract, preferred_element_type=jnp.float32
        )
        one = one_ref[:, part].astype(jnp.float32)
        two = two_ref[:, part].astype(jnp.float32)
        upper = jnp.where(one_first, one, two)
        lower = jnp.where(one_first, two, one)
        moment, before, weights = [
            jnp.concatenate([upper[r : r + 4], lower[r : r + 4]], axis=0) for r in (0, 4, 8)
        ]
        _, _, update = moments((both[:8] + both[8:]) / 256, weights, moment, before)
        update_ref[:, part] = update
        kept_ref[:, part] = weights
        weight_sq = weight_sq + weights * weights
        update_sq = update_sq + update * update
    row = lax.broadcasted_iota(jnp.int32, (8, 128), 0)
    lane = lax.broadcasted_iota(jnp.int32, (8, 128), 1)
    notes = jnp.where(
        (row == 0) & (lane == 0),
        jnp.sum(weight_sq),
        jnp.where((row == 0) & (lane == 1), jnp.sum(update_sq), 0.0),
    )
    for core in range(2):
        rows = slice(4 * core, 4 * core + 4)
        sent = jnp.concatenate([first[rows], second[rows]], axis=0)
        for place in range(16):
            message_ref[2 * place + core, 0:8, :] = sent
            message_ref[2 * place + core, 8:16, :] = notes


def rows_kernel(
    at_ref, inbox_ref, update_ref, kept_ref, rows_ref, ratio_ref, own_left_ref, other_left_ref
):
    sketch = inbox_ref[at_ref[2], 0:8, :]
    swapped = jnp.concatenate([sketch[4:8], sketch[0:4]], axis=0)
    mine_first = jnp.where(at_ref[0] == 0, sketch, swapped)
    high = mine_first.astype(jnp.bfloat16).astype(jnp.float32)
    rest = mine_first - high
    middle = rest.astype(jnp.bfloat16).astype(jnp.float32)
    parts = (high, middle, rest - middle)
    for ref, rows in ((own_left_ref, slice(0, 4)), (other_left_ref, slice(4, 8))):
        ref[...] = jnp.concatenate([p[rows] for p in parts], axis=0).astype(jnp.bfloat16)
    notes = inbox_ref[0, 8:16, :]
    for source in range(1, 32):
        notes = notes + inbox_ref[source, 8:16, :]
    lane = lax.broadcasted_iota(jnp.int32, (8, 128), 1)
    weight_sq = jnp.sum(jnp.where(lane == 0, notes, 0.0), keepdims=True)
    update_sq = jnp.sum(jnp.where(lane == 1, notes, 0.0), keepdims=True)
    ratio = jnp.sqrt(weight_sq) / (jnp.sqrt(update_sq) + norm_eps)
    ratio_ref[...] = jnp.broadcast_to(ratio, (8, 128))
    for start in range(0, update_ref.shape[1], CHUNK):
        part = pl.ds(start, CHUNK)
        rows = (kept_ref[:, part] - rate * ratio * update_ref[:, part]).astype(jnp.bfloat16)
        for place in range(16):
            rows_ref[place, :, part] = rows


def place_kernel(which, at_ref, rows_ref, *refs):
    out_ref, sems = refs[-2:]
    copies = [
        pltpu.make_async_copy(
            rows_ref.at[i],
            out_ref.at[i % 2 * 8 + i // 2 % 2 * 4 + i // 4, at_ref[which]],
            sems.at[i],
        )
        for i in range(16)
    ]
    for copy in copies:
        copy.start()
    for copy in copies:
        copy.wait()


def place(which, at, rows, *partly):
    shape = (16, 2) + rows.shape[1:]
    return pl.pallas_call(
        functools.partial(place_kernel, which),
        out_shape=jax.ShapeDtypeStruct(shape, rows.dtype),
        in_specs=[SMEM, VMEM] + [pl.BlockSpec(memory_space=pl.ANY)] * len(partly),
        out_specs=pl.BlockSpec(memory_space=pl.ANY),
        scratch_shapes=[pltpu.SemaphoreType.DMA((16,))],
        input_output_aliases={2: 0} if partly else {},
        cost_estimate=pl.CostEstimate(flops=0, bytes_accessed=2 * rows.nbytes, transcendentals=0),
        compiler_params=LIMIT,
        name="place",
    )(at, rows, *partly)


def on_device(grads, basis, weights, moment, second):
    grad = grads[0, 0, 0]
    width = grad.shape[1]
    core = lax.axis_index("c")
    deep = lax.axis_index("z")
    low = lax.axis_index("yl")
    outer = lax.axis_index("yh") * 4 + lax.axis_index("x")

    turned = basis.T
    half = turned.shape[1] // 2
    mine = lax.dynamic_slice_in_dim(turned, half * core, half, 1)
    theirs = swap(lax.dynamic_slice_in_dim(turned, half * (1 - core), half, 1))
    chip = in_order(core, mine, theirs, 0).reshape(-1, half)
    part = chip.shape[0] // 8
    piece = lax.dynamic_slice_in_dim(chip, part * outer, part, 0)
    at = jnp.stack([core, (2 * outer + core + deep) % 16 // 8, low * 16 + deep, 1 - core])
    piece, at = lax.optimization_barrier((piece, at.astype(jnp.int32)))
    along_z = share(piece, "z", 16)
    along_z, m_in, v_in, w_in = lax.optimization_barrier((along_z, moment, second, weights))
    state = pl.pallas_call(
        pack_kernel,
        out_shape=jax.ShapeDtypeStruct((12, width), jnp.bfloat16),
        in_specs=[VMEM, VMEM, VMEM],
        out_specs=VMEM,
        compiler_params=LIMIT,
        name="pack",
    )(m_in, v_in, w_in)
    came_one = lax.ppermute(state, ALL, along_z_moves(0))
    other_grad = swap(grad)
    blocks = share(along_z, X_FIRST, 16)
    blocks, came_one = lax.optimization_barrier((blocks, came_one))
    blocks = blocks.reshape(4, 2, 2, 16, part, half)
    own_basis = blocks.transpose(2, 3, 1, 0, 4, 5).reshape(width, half)

    sketch = pl.pallas_call(
        product_kernel,
        out_shape=jax.ShapeDtypeStruct((grad.shape[0], half), jnp.float32),
        in_specs=[VMEM, VMEM, VMEM],
        out_specs=VMEM,
        compiler_params=LIMIT,
        name="product",
    )(grad, other_grad, own_basis)
    sketch, state, came_one = lax.optimization_barrier((sketch, state, came_one))
    came_two = lax.ppermute(state, ALL, along_z_moves(1))
    state_one = lax.ppermute(came_one, ALL, in_plane_moves(0))
    plane_terms = exchange(sketch.reshape(16, 16, half), PLANE)
    plane_terms, came_two, basis_sent = lax.optimization_barrier(
        (plane_terms, came_two, own_basis)
    )
    other_basis = swap(basis_sent)
    plane_sum = jnp.sum(plane_terms, axis=0)
    state_two = lax.ppermute(came_two, ALL, in_plane_moves(1))
    spread = jnp.broadcast_to(plane_sum.reshape(2, 1, 8, half), (2, 16, 8, half))
    terms = exchange(spread.reshape(32, 8, half), ("c", "z"))

    wide = jax.ShapeDtypeStruct((8, width), jnp.float32)
    update8, kept8, message = pl.pallas_call(
        update_kernel,
        out_shape=(wide, wide, jax.ShapeDtypeStruct((32, 16, half), jnp.float32)),
        in_specs=[SMEM, VMEM, VMEM, VMEM, VMEM, VMEM],
        out_specs=(VMEM, VMEM, VMEM),
        compiler_params=LIMIT,
        name="update",
    )(
        at,
        terms,
        own_basis,
        other_basis,
        state_one,
        state_two,
    )
    inbox = exchange(message, PLANE + ("c",))
    left = jax.ShapeDtypeStruct((12, half), jnp.bfloat16)
    rows_out, ratio, own_left, other_left = pl.pallas_call(
        rows_kernel,
        out_shape=(
            jax.ShapeDtypeStruct((16, 8, width), jnp.bfloat16),
            jax.ShapeDtypeStruct((8, 128), jnp.float32),
            left,
            left,
        ),
        in_specs=[SMEM, VMEM, VMEM, VMEM],
        out_specs=(VMEM, VMEM, VMEM, VMEM),
        compiler_params=LIMIT,
        name="rows",
    )(at, inbox, update8, kept8)
    rows_mine = exchange(rows_out, X_FIRST)
    rows_mine, ratio, own_left, other_left = lax.optimization_barrier(
        (rows_mine, ratio, own_left, other_left)
    )
    rows_other = swap(rows_mine)
    gathered = place(3, at, rows_other, place(0, at, rows_mine)).reshape(1, 256, width)

    trust_ratio = ratio[0, 0]
    turn = (((1,), (1,)), ((), ()))
    estimate = lax.dot_general(own_left, own_basis, turn, preferred_element_type=jnp.float32)
    estimate = estimate + lax.dot_general(
        other_left, other_basis, turn, preferred_element_type=jnp.float32
    )
    estimate = (estimate[0:4] + estimate[4:8] + estimate[8:12])[None] / 256
    moment_new, second_new, update = moments(estimate, weights, moment, second)
    weight_new = weights - rate * trust_ratio * update
    return (weight_new, moment_new, second_new, gathered)


def solution(mesh):
    fine = Mesh(mesh.devices.reshape(tuple(FINE.values())), tuple(FINE))
    rows = P(None, DP, None)
    return jax.shard_map(
        on_device,
        mesh=fine,
        in_specs=(P(OUTER, DP, None, None, None), P(None, DP), rows, rows, rows),
        out_specs=(rows, rows, rows, P()),
        check_vma=False,
    )
```

```python
import functools

import jax
import jax.numpy as jnp
from jax import lax
from jax.experimental import pallas as pl
from jax.experimental.pallas import tpu as pltpu
from jax.sharding import Mesh
from jax.sharding import PartitionSpec as P

beta_one = 0.9
beta_two = 0.999
bias_one = 1.0 - 0.9**10
bias_two = 1.0 - 0.999**10
adam_eps = 1e-06
norm_eps = 1e-06
decay = 0.01
rate = 0.1

FINE = {"yh": 2, "x": 4, "yl": 2, "z": 16, "c": 2}
OUTER = ("yh", "x")
DP = ("yl", "z", "c")
PLANE = ("yl", "yh", "x")
X_FIRST = ("x", "yh", "yl")
SWAP = [(0, 1), (1, 0)]
ALL = tuple(FINE)


def moves(target):
    pairs = []
    for o in range(8):
        for low in range(2):
            for z in range(16):
                for c in range(2):
                    to_o, to_z, to_c = target(o, z, c)
                    pairs.append(
                        (((o * 2 + low) * 16 + z) * 2 + c, ((to_o * 2 + low) * 16 + to_z) * 2 + to_c)
                    )
    return pairs


def along_z_moves(first):
    return moves(lambda o, z, c: (o, (o + 8 * ((c + first) % 2) - z) % 16, c))


def in_plane_moves(first):
    def target(o, z, c):
        row = (o + 8 * ((c + first) % 2) - z) % 16
        return row // 2, z, row % 2

    return moves(target)


def exchange(blocks, axes):
    return lax.all_to_all(blocks, axes, 0, 0, tiled=True)


def share(block, axes, count):
    return exchange(jnp.broadcast_to(block[None], (count,) + block.shape), axes)


def swap(block):
    return lax.ppermute(block, "c", SWAP)


def in_order(position, mine, other, axis):
    shape = [1] * (mine.ndim + 1)
    shape[axis] = 2
    here = (jnp.arange(2) == position).reshape(shape)
    return jnp.where(here, jnp.expand_dims(mine, axis), jnp.expand_dims(other, axis))


def moments(estimate, weights, moment, second):
    moment_new = beta_one * moment + (1.0 - beta_one) * estimate
    second_new = beta_two * second + (1.0 - beta_two) * estimate * estimate
    update = moment_new / bias_one / (jnp.sqrt(second_new / bias_two) + adam_eps) + decay * weights
    return moment_new, second_new, update


VMEM = pl.BlockSpec(memory_space=pltpu.VMEM)
SMEM = pl.BlockSpec(memory_space=pltpu.SMEM)
LIMIT = pltpu.CompilerParams(vmem_limit_bytes=6 << 20)
CHUNK = 512


def pack_kernel(moment_ref, second_ref, weights_ref, out_ref):
    rows = [moment_ref[0], second_ref[0], weights_ref[0]]
    out_ref[...] = jnp.concatenate(rows, axis=0).astype(jnp.bfloat16)


def product_kernel(grad_ref, other_ref, basis_ref, out_ref):
    basis = basis_ref[...]
    total = jnp.dot(grad_ref[...], basis, preferred_element_type=jnp.float32)
    out_ref[...] = total + jnp.dot(other_ref[...], basis, preferred_element_type=jnp.float32)


def update_kernel(
    at_ref, terms_ref, own_ref, other_ref, one_ref, two_ref, update_ref, kept_ref, message_ref
):
    first, second = terms_ref[0], terms_ref[16]
    for step in range(1, 16):
        first = first + terms_ref[step]
        second = second + terms_ref[16 + step]
    at_first = at_ref[0] == 0
    one_first = at_ref[1] == 0

    def left_of(half):
        high = half.astype(jnp.bfloat16).astype(jnp.float32)
        return jnp.concatenate([high, half - high], axis=0).astype(jnp.bfloat16)

    left_own = left_of(jnp.where(at_first, first, second))
    left_other = left_of(jnp.where(at_first, second, first))
    contract = (((1,), (1,)), ((), ()))
    weight_sq = jnp.zeros((8, CHUNK), jnp.float32)
    update_sq = jnp.zeros((8, CHUNK), jnp.float32)
    for start in range(0, own_ref.shape[0], CHUNK):
        part = pl.ds(start, CHUNK)
        both = lax.dot_general(
            left_own, own_ref[part, :], contract, preferred_element_type=jnp.float32
        ) + lax.dot_general(
            left_other, other_ref[part, :], contract, preferred_element_type=jnp.float32
        )
        one = one_ref[:, part].astype(jnp.float32)
        two = two_ref[:, part].astype(jnp.float32)
        upper = jnp.where(one_first, one, two)
        lower = jnp.where(one_first, two, one)
        moment, before, weights = [
            jnp.concatenate([upper[r : r + 4], lower[r : r + 4]], axis=0) for r in (0, 4, 8)
        ]
        _, _, update = moments((both[:8] + both[8:]) / 256, weights, moment, before)
        update_ref[:, part] = update
        kept_ref[:, part] = weights
        weight_sq = weight_sq + weights * weights
        update_sq = update_sq + update * update
    row = lax.broadcasted_iota(jnp.int32, (8, 128), 0)
    lane = lax.broadcasted_iota(jnp.int32, (8, 128), 1)
    notes = jnp.where(
        (row == 0) & (lane == 0),
        jnp.sum(weight_sq),
        jnp.where((row == 0) & (lane == 1), jnp.sum(update_sq), 0.0),
    )
    for core in range(2):
        rows = slice(4 * core, 4 * core + 4)
        sent = jnp.concatenate([first[rows], second[rows]], axis=0)
        for place in range(16):
            message_ref[2 * place + core, 0:8, :] = sent
            message_ref[2 * place + core, 8:16, :] = notes


def rows_kernel(
    at_ref, inbox_ref, update_ref, kept_ref, rows_ref, ratio_ref, own_left_ref, other_left_ref
):
    sketch = inbox_ref[at_ref[2], 0:8, :]
    swapped = jnp.concatenate([sketch[4:8], sketch[0:4]], axis=0)
    mine_first = jnp.where(at_ref[0] == 0, sketch, swapped)
    high = mine_first.astype(jnp.bfloat16).astype(jnp.float32)
    rest = mine_first - high
    middle = rest.astype(jnp.bfloat16).astype(jnp.float32)
    parts = (high, middle, rest - middle)
    for ref, rows in ((own_left_ref, slice(0, 4)), (other_left_ref, slice(4, 8))):
        ref[...] = jnp.concatenate([p[rows] for p in parts], axis=0).astype(jnp.bfloat16)
    notes = inbox_ref[0, 8:16, :]
    for source in range(1, 32):
        notes = notes + inbox_ref[source, 8:16, :]
    lane = lax.broadcasted_iota(jnp.int32, (8, 128), 1)
    weight_sq = jnp.sum(jnp.where(lane == 0, notes, 0.0), keepdims=True)
    update_sq = jnp.sum(jnp.where(lane == 1, notes, 0.0), keepdims=True)
    ratio = jnp.sqrt(weight_sq) / (jnp.sqrt(update_sq) + norm_eps)
    ratio_ref[...] = jnp.broadcast_to(ratio, (8, 128))
    for start in range(0, update_ref.shape[1], CHUNK):
        part = pl.ds(start, CHUNK)
        rows = (kept_ref[:, part] - rate * ratio * update_ref[:, part]).astype(jnp.bfloat16)
        for place in range(16):
            rows_ref[place, :, part] = rows


def place_kernel(which, at_ref, rows_ref, *refs):
    out_ref, sems = refs[-2:]
    copies = [
        pltpu.make_async_copy(
            rows_ref.at[i],
            out_ref.at[i % 2 * 8 + i // 2 % 2 * 4 + i // 4, at_ref[which]],
            sems.at[i],
        )
        for i in range(16)
    ]
    for copy in copies:
        copy.start()
    for copy in copies:
        copy.wait()


def place(which, at, rows, *partly):
    shape = (16, 2) + rows.shape[1:]
    return pl.pallas_call(
        functools.partial(place_kernel, which),
        out_shape=jax.ShapeDtypeStruct(shape, rows.dtype),
        in_specs=[SMEM, VMEM] + [pl.BlockSpec(memory_space=pl.ANY)] * len(partly),
        out_specs=pl.BlockSpec(memory_space=pl.ANY),
        scratch_shapes=[pltpu.SemaphoreType.DMA((16,))],
        input_output_aliases={2: 0} if partly else {},
        cost_estimate=pl.CostEstimate(flops=0, bytes_accessed=2 * rows.nbytes, transcendentals=0),
        compiler_params=LIMIT,
        name="place",
    )(at, rows, *partly)


def on_device(grads, basis, weights, moment, second):
    grad = grads[0, 0, 0]
    width = grad.shape[1]
    core = lax.axis_index("c")
    deep = lax.axis_index("z")
    low = lax.axis_index("yl")
    outer = lax.axis_index("yh") * 4 + lax.axis_index("x")

    turned = basis.T
    half = turned.shape[1] // 2
    mine = lax.dynamic_slice_in_dim(turned, half * core, half, 1)
    theirs = swap(lax.dynamic_slice_in_dim(turned, half * (1 - core), half, 1))
    chip = in_order(core, mine, theirs, 0).reshape(-1, half)
    part = chip.shape[0] // 8
    piece = lax.dynamic_slice_in_dim(chip, part * outer, part, 0)
    at = jnp.stack([core, (2 * outer + core + deep) % 16 // 8, low * 16 + deep, 1 - core])
    piece, at = lax.optimization_barrier((piece, at.astype(jnp.int32)))
    along_z = share(piece, "z", 16)
    along_z, m_in, v_in, w_in = lax.optimization_barrier((along_z, moment, second, weights))
    state = pl.pallas_call(
        pack_kernel,
        out_shape=jax.ShapeDtypeStruct((12, width), jnp.bfloat16),
        in_specs=[VMEM, VMEM, VMEM],
        out_specs=VMEM,
        compiler_params=LIMIT,
        name="pack",
    )(m_in, v_in, w_in)
    came_one = lax.ppermute(state, ALL, along_z_moves(0))
    other_grad = swap(grad)
    blocks = share(along_z, X_FIRST, 16)
    blocks, came_one = lax.optimization_barrier((blocks, came_one))
    blocks = blocks.reshape(4, 2, 2, 16, part, half)
    own_basis = blocks.transpose(2, 3, 1, 0, 4, 5).reshape(width, half)

    sketch = pl.pallas_call(
        product_kernel,
        out_shape=jax.ShapeDtypeStruct((grad.shape[0], half), jnp.float32),
        in_specs=[VMEM, VMEM, VMEM],
        out_specs=VMEM,
        compiler_params=LIMIT,
        name="product",
    )(grad, other_grad, own_basis)
    sketch, state, came_one = lax.optimization_barrier((sketch, state, came_one))
    came_two = lax.ppermute(state, ALL, along_z_moves(1))
    state_one = lax.ppermute(came_one, ALL, in_plane_moves(0))
    plane_terms = exchange(sketch.reshape(16, 16, half), PLANE)
    plane_terms, came_two, state_one, basis_sent = lax.optimization_barrier(
        (plane_terms, came_two, state_one, own_basis)
    )
    other_basis = swap(basis_sent)
    plane_sum = jnp.sum(plane_terms, axis=0)
    state_two = lax.ppermute(came_two, ALL, in_plane_moves(1))
    spread = jnp.broadcast_to(plane_sum.reshape(2, 1, 8, half), (2, 16, 8, half))
    terms = exchange(spread.reshape(32, 8, half), ("c", "z"))

    wide = jax.ShapeDtypeStruct((8, width), jnp.float32)
    update8, kept8, message = pl.pallas_call(
        update_kernel,
        out_shape=(wide, wide, jax.ShapeDtypeStruct((32, 16, half), jnp.float32)),
        in_specs=[SMEM, VMEM, VMEM, VMEM, VMEM, VMEM],
        out_specs=(VMEM, VMEM, VMEM),
        compiler_params=LIMIT,
        name="update",
    )(
        at,
        terms,
        own_basis,
        other_basis,
        state_one,
        state_two,
    )
    inbox = exchange(message, PLANE + ("c",))
    left = jax.ShapeDtypeStruct((12, half), jnp.bfloat16)
    rows_out, ratio, own_left, other_left = pl.pallas_call(
        rows_kernel,
        out_shape=(
            jax.ShapeDtypeStruct((16, 8, width), jnp.bfloat16),
            jax.ShapeDtypeStruct((8, 128), jnp.float32),
            left,
            left,
        ),
        in_specs=[SMEM, VMEM, VMEM, VMEM],
        out_specs=(VMEM, VMEM, VMEM, VMEM),
        compiler_params=LIMIT,
        name="rows",
    )(at, inbox, update8, kept8)
    rows_mine = exchange(rows_out, X_FIRST)
    rows_mine, ratio, own_left, other_left = lax.optimization_barrier(
        (rows_mine, ratio, own_left, other_left)
    )
    rows_other = swap(rows_mine)
    gathered = place(3, at, rows_other, place(0, at, rows_mine)).reshape(1, 256, width)

    trust_ratio = ratio[0, 0]
    turn = (((1,), (1,)), ((), ()))
    estimate = lax.dot_general(own_left, own_basis, turn, preferred_element_type=jnp.float32)
    estimate = estimate + lax.dot_general(
        other_left, other_basis, turn, preferred_element_type=jnp.float32
    )
    estimate = (estimate[0:4] + estimate[4:8] + estimate[8:12])[None] / 256
    moment_new, second_new, update = moments(estimate, weights, moment, second)
    weight_new = weights - rate * trust_ratio * update
    return (weight_new, moment_new, second_new, gathered)


def solution(mesh):
    fine = Mesh(mesh.devices.reshape(tuple(FINE.values())), tuple(FINE))
    rows = P(None, DP, None)
    return jax.shard_map(
        on_device,
        mesh=fine,
        in_specs=(P(OUTER, DP, None, None, None), P(None, DP), rows, rows, rows),
        out_specs=(rows, rows, rows, P()),
        check_vma=False,
    )
```
